256 devices in a mesh: blk: 32 (over z, y_hi, core), slab: 8 (over x, y_lo).
Axes of the slice: x: 4, y: 4 (y_hi: 2, y_lo: 2; y = y_hi * 2 + y_lo), z: 8, core: 2. Of those that a mesh axis runs over, the one named last changes fastest.
Arguments:
- queries: bfloat16 [512, 768], P('blk'), may hold values from -64 to 64
- teacher_weight: bfloat16 [512, 200], P('blk'), may hold values from 0.0009994507 to 1
- cand_ids: int32 [512, 200], P('blk'), may hold values from 0 to 262143, as said below
- passages: bfloat16 [262144, 768], P(('blk', 'slab')), may hold values from -8 to 8
Outputs:
- loss: float32 [512], P('blk')
- grad_query: float32 [512, 768], P(('blk', 'slab'))
The draws below stay inside these ranges and needn't reach their ends.
Inputs may be any that keep to these rules, and one draw needn't show every extreme that they name: `cand_ids`: each row holds 200 distinct ids; the k-th lies in the k-th of 200 consecutive ranges of 1310 ids (the last range runs to the end).
All inputs are finite; a program needn't handle non-finite values.
Results may differ from the reference program's by a relative error of at most 0.012.
Values may be sent and summed in bfloat16 or wider, within the bound.
A program may use at most 64 MiB of HBM per device.

```python
import math
import jax
import jax.numpy as jnp
from jax import lax

D = 768
CAND = 200
NP_DEV = 1024
NQ = 512
NP = 262144


def common_vector(key, spread):
    shared = jax.random.normal(jax.random.fold_in(key, 17), (D,), jnp.float32)
    return jnp.clip(spread * shared, -3.0, 3.0)


def passage_row(pkey, common, row):
    rkey = jax.random.fold_in(pkey, row)
    base = jnp.clip(jax.random.normal(rkey, (D,), jnp.float32), -4.0, 4.0)
    rough = jax.random.uniform(jax.random.fold_in(rkey, 7), (), jnp.float32, 0.8, 1.2)
    rising = 1.0 + 0.15 * row.astype(jnp.float32) / NP
    return base * rough * rising + common


def draw_passages(key, part):
    common = common_vector(key, 1.2)
    pkey = jax.random.fold_in(key, 11)
    rows = jax.vmap(lambda r: passage_row(pkey, common, r))(jnp.arange(NP, dtype=jnp.int32))
    return jnp.clip(rows, -8.0, 8.0).astype(jnp.bfloat16)


def draw_queries(key, part):
    qkey = jax.random.fold_in(key, 12)
    values = 0.5 * jnp.clip(jax.random.normal(qkey, (NQ, D), jnp.float32), -5.0, 5.0)
    return jnp.clip(values, -64.0, 64.0).astype(jnp.bfloat16)


def draw_cand_ids(key, part):
    stride = NP // CAND
    offsets = jax.random.randint(jax.random.fold_in(key, 14), (NQ, CAND), 0, stride)
    last = jax.random.randint(jax.random.fold_in(key, 15), (NQ,), 0, NP - (CAND - 1) * stride)
    offsets = offsets.at[:, CAND - 1].set(last)
    ids = jnp.arange(CAND, dtype=jnp.int32)[None, :] * stride + offsets
    ids = ids.at[0, CAND - 1].set(NP - 1)
    ids = ids.at[1, 0].set(0)
    return ids.astype(jnp.int32)


def block_scale(rng, dims, pieces, least, largest):
    def one(dim, shards_of):
        draws = jax.random.uniform(jax.random.fold_in(jax.random.fold_in(rng, 6), dim), (shards_of,), jnp.float32, least / len(pieces), largest / len(pieces))
        return jnp.repeat(jnp.exp(draws), dims[dim] // shards_of).reshape((-1,) + (1,) * (len(dims) - dim - 1))

    level = one(*pieces[0])
    for cut in pieces[1:]:
        level = level * one(*cut)
    return level


def setup_inputs(seed: int = 0) -> dict:
    key_list = jax.random.split(jax.random.key(seed), 5)
    return {
        "queries": draw_queries(jax.random.fold_in(key_list[4], 71), 0),
        "teacher_weight": jnp.clip(jnp.exp(math.log(1.0) - 6.9083047 * jax.random.uniform(key_list[1], (NQ, CAND), jnp.float32) ** block_scale(key_list[1], (NQ, CAND), ((0, 32),), -0.2, 0.2)), 0.0009994507, 1.0).astype(jnp.bfloat16),
        "cand_ids": draw_cand_ids(jax.random.fold_in(key_list[4], 71), 0),
        "passages": draw_passages(jax.random.fold_in(key_list[4], 71), 0),
    }


def block_target(cand_ids, tprob, start, width):
    local_ids = cand_ids - start
    inside = (local_ids >= 0) & (local_ids < width)
    safe_ids = jnp.where(inside, local_ids, 0).astype(jnp.int32)
    row_ids = jnp.broadcast_to(jnp.arange(cand_ids.shape[0], dtype=jnp.int32)[:, None], cand_ids.shape)
    dense = jnp.zeros((cand_ids.shape[0], width), jnp.float32)
    dense = dense.at[row_ids, safe_ids].add(jnp.where(inside, tprob, jnp.float32(0.0)))
    return (dense, inside, safe_ids)

def reference(queries, teacher_weight, cand_ids, passages):
    logit_scale = 3.0 / math.sqrt(D)
    width = NP_DEV
    blocks = NP // width
    weights = teacher_weight.astype(jnp.float32)
    tprob = weights / lax.optimization_barrier(jnp.sum(weights, axis=1, keepdims=True))

    def block_scores(index):
        start = (index * width).astype(jnp.int32)
        piece = lax.dynamic_slice_in_dim(passages, start, width, 0)
        scores = logit_scale * lax.dot_general(queries, piece, (((1,), (1,)), ((), ())), preferred_element_type=jnp.float32)
        return (scores, piece, start)

    def first_pass(carry, index):
        peak, total, teacher_sum = carry
        scores, piece, start = block_scores(index)
        local_ids = cand_ids - start
        inside = (local_ids >= 0) & (local_ids < width)
        safe_ids = jnp.where(inside, local_ids, 0).astype(jnp.int32)
        picked = jnp.take_along_axis(scores, safe_ids, axis=1)
        teacher_sum = teacher_sum + lax.optimization_barrier(jnp.sum(jnp.where(inside, tprob * picked, jnp.float32(0.0)), axis=1))
        new_peak = jnp.maximum(peak, lax.optimization_barrier(jnp.max(scores, axis=1)))
        total = total * jnp.exp(peak - new_peak) + lax.optimization_barrier(jnp.sum(jnp.exp(scores - new_peak[:, None]), axis=1))
        return ((new_peak, total, teacher_sum), None)
    rows = queries.shape[0]
    init = (jnp.full((rows,), -jnp.inf, jnp.float32), jnp.zeros((rows,), jnp.float32), jnp.zeros((rows,), jnp.float32))
    (peak, total, teacher_sum), _ = lax.scan(first_pass, init, jnp.arange(blocks, dtype=jnp.int32))
    lse = peak + jnp.log(total)
    loss = lax.optimization_barrier(jnp.sum(tprob * jnp.log(tprob), axis=1)) - teacher_sum + lse

    def second_pass(acc, index):
        scores, piece, start = block_scores(index)
        dense, inside, safe_ids = block_target(cand_ids, tprob, start, width)
        delta = (jnp.exp(scores - lse[:, None]) - dense).astype(jnp.bfloat16)
        return (acc + jnp.dot(delta, piece, preferred_element_type=jnp.float32), None)
    grad, _ = lax.scan(second_pass, jnp.zeros((rows, D), jnp.float32), jnp.arange(blocks, dtype=jnp.int32))
    return (loss, logit_scale * grad)
```

```python
import functools
import math

import jax
import jax.numpy as jnp
from jax import lax
from jax.experimental import pallas as pl
from jax.experimental.pallas import tpu as pltpu
from jax.sharding import PartitionSpec as P

MESH = pl.DeviceIdType.MESH
F32 = jnp.float32
BF16 = jnp.bfloat16
I32 = jnp.int32
FAR_FIRST = (4, 3, 5, 2, 6, 1, 7, 0)


def position():
    blk = lax.axis_index("blk")
    slab = lax.axis_index("slab")
    z = blk // 4
    y = ((blk // 2) % 2) * 2 + slab % 2
    return slab // 2, y, z, blk % 2


def device(x, y, z, core):
    return {"blk": (z * 2 + y // 2) * 2 + core, "slab": x * 2 + y % 2}


def iota(shape, dim):
    return lax.broadcasted_iota(I32, shape, dim)


def split3(value):
    first = value.astype(BF16)
    rest = value - first.astype(F32)
    second = rest.astype(BF16)
    third = (rest - second.astype(F32)).astype(BF16)
    return first, second, third


def kernel(
    stride,
    scale,
    q_ref,
    w_ref,
    id_ref,
    pas_ref,
    loss_ref,
    grad_ref,
    pas,
    queries,
    cands,
    cand_out,
    perm_ref,
    prob_out,
    exp_out,
    stat_out,
    prob_in,
    exp_in,
    stat_in,
    z_out,
    z_in,
    zstat_out,
    zstat_in,
    pas_sem,
    q_sems,
    c_sems,
    prob_sems,
    exp_sems,
    stat_sems,
    z_sems,
    zstat_sems,
):
    x, y, z, core = position()
    y_hi, y_lo = y // 2, y % 2
    slab = x * 2 + y_lo
    width = pas_ref.shape[0]
    num_cand = id_ref.shape[1]
    plane = width * 32
    per_plane = plane // stride

    gather_to = [
        (device(x, y if dy == 0 else 3 - y, (z + d) % 8, core), dy * 8 + (8 - d) % 8, d)
        for d in FAR_FIRST
        for dy in (0, 1)
        if (d, dy) != (0, 0)
    ]
    plane_to = [
        (
            device((x + ex) % 4, (y + ey) % 4, z, core),
            ex * 4 + ey,
            ((4 - ex) % 4) * 4 + (4 - ey) % 4,
            (((y + ey) % 4) // 2 + y_hi) % 2,
        )
        for ex in (2, 1, 3, 0)
        for ey in (2, 1, 3, 0)
        if (ex, ey) != (0, 0)
    ]
    z_to = [(device(x, y, (z + d) % 8, core), d, (8 - d) % 8) for d in FAR_FIRST if d]
    other = device(x, y, z, 1 - core)

    barrier = pltpu.get_barrier_semaphore()
    greeted = [other] + [p[0] for p in plane_to]
    greeted += [p[0] for p in gather_to if p[2] != 0]
    for target in greeted:
        pl.semaphore_signal(barrier, inc=1, device_id=target, device_id_type=MESH)

    load = pltpu.make_async_copy(pas_ref, pas.at[0], pas_sem.at[0])
    load.start()

    weights = w_ref[...].astype(F32)
    weight_sum = jnp.sum(weights, axis=1, keepdims=True)
    own_prob = weights / weight_sum
    entropy = jnp.sum(own_prob * jnp.log(own_prob), axis=1, keepdims=True)
    pad = 256 - num_cand
    wide_w = jnp.concatenate([weights, jnp.zeros((16, pad), F32)], axis=1)
    wide_id = jnp.concatenate([id_ref[...], jnp.zeros((16, pad), I32)], axis=1)
    s1, s2, s3 = split3(weight_sum)
    lane32 = iota((16, 32), 1)
    sums = jnp.where(
        lane32 == 0,
        s1.astype(F32),
        jnp.where(lane32 == 1, s2.astype(F32), jnp.where(lane32 == 2, s3.astype(F32), 0.0)),
    )
    for zz in range(8):
        lo = per_plane * zz
        ids = jnp.maximum(wide_id[:, lo : lo + 32] - lo * stride, 0)
        high = (ids >> 8).astype(F32)
        low = (ids & 255).astype(F32)
        cand_out[zz] = jnp.concatenate([high, low, wide_w[:, lo : lo + 32], sums], axis=1).astype(BF16)
    cands[0] = cand_out[z]
    queries[0] = q_ref[...]

    p_row = iota((256, 1), 0)
    p_x = (x + (p_row >> 6)) & 3
    p_y = (y + ((p_row >> 4) & 3)) & 3
    p_dy = ((p_y >> 1) + y_hi) & 1
    p_n = p_dy * 128 + ((p_row >> 1) & 7) * 16 + (p_x * 2 + (p_y & 1)) * 2 + (p_row & 1)
    hot = (iota((256, 256), 1) == p_n).astype(F32)
    perm_ref[...] = hot.astype(BF16)

    pl.semaphore_wait(barrier, len(greeted))

    swap = pltpu.make_async_remote_copy(
        pas_ref, pas.at[1], pas_sem.at[1], pas_sem.at[2], device_id=other, device_id_type=MESH
    )
    swap.start()
    sent = []
    cand_copies, q_copies = {}, {}
    for i, (target, slot, d) in enumerate(gather_to):
        copy = pltpu.make_async_remote_copy(
            cand_out.at[(z + d) % 8],
            cands.at[slot],
            c_sems.at[0, i],
            c_sems.at[1, i],
            device_id=target,
            device_id_type=MESH,
        )
        copy.start()
        cand_copies[i] = copy
    for i, (target, slot, d) in enumerate(gather_to):
        copy = pltpu.make_async_remote_copy(
            q_ref,
            queries.at[slot],
            q_sems.at[0, i],
            q_sems.at[1, i],
            device_id=target,
            device_id_type=MESH,
        )
        copy.start()
        q_copies[i] = copy
    sent += list(cand_copies.values()) + list(q_copies.values())

    offsets = [((((z * 2 + y_hi) * 2 + c) * 8) + slab) * width for c in (core, 1 - core)]
    firsts = [jnp.minimum(off // stride, num_cand - 2) - per_plane * z for off in offsets]
    out_lane = iota((1, 128), 1)
    target_lane = jnp.where((out_lane >= 12) & (out_lane < 15), 96 + out_lane - 12, -1)
    for rho in range(2):
        for c in range(2):
            for field in range(3):
                target_lane = jnp.where(
                    out_lane == (rho * 2 + c) * 3 + field, field * 32 + firsts[rho] + c, target_lane
                )
    pick = (iota((128, 128), 0) == target_lane).astype(F32).astype(BF16)
    for copy in cand_copies.values():
        copy.wait_recv()
    picked = jnp.dot(cands[...].reshape(256, 128), pick, preferred_element_type=F32).astype(BF16)
    picked = jnp.dot(perm_ref[...], picked, preferred_element_type=F32)
    total_w = picked[:, 12:13] + picked[:, 13:14] + picked[:, 14:15]
    load.wait()
    column = iota((256, width), 1).astype(F32)
    prob_sum = None
    swap.wait_recv()
    for rho in range(2):
        shift = (per_plane * stride * z - offsets[rho]).astype(F32)
        dense = None
        for c in range(2):
            at = (rho * 2 + c) * 3
            local = picked[:, at : at + 1] * 256.0 + picked[:, at + 1 : at + 2] + shift
            prob = picked[:, at + 2 : at + 3] / total_w
            term = jnp.where(column == local, prob, 0.0)
            dense = term if dense is None else dense + term
        part = jnp.dot(dense.astype(BF16), pas[rho], preferred_element_type=F32)
        prob_sum = part if prob_sum is None else prob_sum + part
    prob_out[...] = prob_sum.astype(BF16).reshape(16, 16, -1)
    prob_copies = []
    for i, (target, group, slot, _) in enumerate(plane_to):
        copy = pltpu.make_async_remote_copy(
            prob_out.at[group],
            prob_in.at[slot],
            prob_sems.at[0, i],
            prob_sems.at[1, i],
            device_id=target,
            device_id_type=MESH,
        )
        copy.start()
        prob_copies.append(copy)
    sent += prob_copies

    for copy in q_copies.values():
        copy.wait_recv()
    depth = q_ref.shape[1]
    rows = jnp.dot(perm_ref[...], queries[...].reshape(256, depth), preferred_element_type=F32)
    rows16 = rows.astype(BF16)
    teacher = scale * jnp.sum(rows * prob_sum, axis=1, keepdims=True)
    nt = (((1,), (1,)), ((), ()))
    scores = [
        scale * lax.dot_general(rows16, pas[rho], nt, preferred_element_type=F32) for rho in range(2)
    ]
    peak = jnp.maximum(
        jnp.max(scores[0], axis=1, keepdims=True), jnp.max(scores[1], axis=1, keepdims=True)
    )
    exps = [jnp.exp(s - peak) for s in scores]
    total = jnp.sum(exps[0], axis=1, keepdims=True) + jnp.sum(exps[1], axis=1, keepdims=True)
    mixed = jnp.dot(exps[0].astype(BF16), pas[0], preferred_element_type=F32) + jnp.dot(
        exps[1].astype(BF16), pas[1], preferred_element_type=F32
    )
    exp_out[...] = mixed.astype(BF16).reshape(16, 16, depth)
    mask = perm_ref[...].astype(F32) > 0.5
    for k, stat in enumerate((peak, total, teacher)):
        lanes = jnp.sum(jnp.where(mask, stat, 0.0), axis=0, keepdims=True)
        stat_out[0, k : k + 1, :] = lanes[:, :128]
        stat_out[1, k : k + 1, :] = lanes[:, 128:]
    exp_copies, stat_copies = [], []
    for i, (target, group, slot, dy) in enumerate(plane_to):
        copy = pltpu.make_async_remote_copy(
            stat_out.at[dy],
            stat_in.at[slot],
            stat_sems.at[0, i],
            stat_sems.at[1, i],
            device_id=target,
            device_id_type=MESH,
        )
        copy.start()
        stat_copies.append(copy)
        copy = pltpu.make_async_remote_copy(
            exp_out.at[group],
            exp_in.at[slot],
            exp_sems.at[0, i],
            exp_sems.at[1, i],
            device_id=target,
            device_id_type=MESH,
        )
        copy.start()
        exp_copies.append(copy)
    sent += exp_copies + stat_copies

    stat_in[0] = stat_out[0]
    for copy in prob_copies:
        copy.wait_recv()
    prob_rows = prob_out[0].astype(F32)
    for i in range(1, 16):
        prob_rows = prob_rows + prob_in[i].astype(F32)
    for copy in stat_copies:
        copy.wait_recv()
    peaks = jnp.concatenate([stat_in[i, 0:1, :] for i in range(16)], axis=0)
    totals = jnp.concatenate([stat_in[i, 1:2, :] for i in range(16)], axis=0)
    teachers = jnp.concatenate([stat_in[i, 2:3, :] for i in range(16)], axis=0)
    peak = jnp.max(peaks, axis=0, keepdims=True)
    share = jnp.exp(peaks - peak)
    total = jnp.sum(totals * share, axis=0, keepdims=True)
    teacher = jnp.sum(teachers, axis=0, keepdims=True)
    zstat_out[0:1, :] = peak
    zstat_out[1:2, :] = total
    zstat_out[2:3, :] = teacher
    zstat_copies = []
    for i, (target, d, slot) in enumerate(z_to):
        copy = pltpu.make_async_remote_copy(
            zstat_out,
            zstat_in.at[slot],
            zstat_sems.at[0, i],
            zstat_sems.at[1, i],
            device_id=target,
            device_id_type=MESH,
        )
        copy.start()
        zstat_copies.append(copy)
    row = iota((16, 128), 0)
    own_lane = iota((16, 128), 1) == (row >> 1) * 16 + slab * 2 + (row & 1)
    columns = [
        jnp.sum(jnp.where(own_lane, share[i : i + 1, :], 0.0), axis=1, keepdims=True) for i in range(16)
    ]
    for copy in exp_copies:
        copy.wait_recv()
    exp_rows = exp_out[0].astype(F32) * columns[0]
    for i in range(1, 16):
        exp_rows = exp_rows + exp_in[i].astype(F32) * columns[i]

    stacked = jnp.concatenate(
        [part[:, b * 128 : (b + 1) * 128] for part in (exp_rows, prob_rows) for b in range(6)], axis=0
    ).astype(BF16)
    o = iota((256, 1), 0)
    j = o & 31
    part = (j >= 12).astype(I32)
    jj = j - 12 * part
    source = part * 96 + (jj >> 1) * 16 + (o >> 5) * 2 + (jj & 1)
    source = jnp.where(j < 24, source, -1)
    order = (iota((256, 192), 1) == source).astype(F32).astype(BF16)
    z_out[...] = jnp.dot(order, stacked, preferred_element_type=F32).astype(BF16).reshape(8, 32, 128)
    z_copies = []
    for i, (target, d, slot) in enumerate(z_to):
        copy = pltpu.make_async_remote_copy(
            z_out.at[d],
            z_in.at[slot],
            z_sems.at[0, i],
            z_sems.at[1, i],
            device_id=target,
            device_id_type=MESH,
        )
        copy.start()
        z_copies.append(copy)
    sent += zstat_copies + z_copies

    zstat_in[0] = zstat_out[...]
    entropy_lanes = jnp.sum(
        jnp.where(iota((16, 16), 0) == iota((16, 16), 1), entropy, 0.0), axis=0, keepdims=True
    )
    for copy in zstat_copies:
        copy.wait_recv()

    def gathered(k):
        return jnp.concatenate(
            [zstat_in[s, k : k + 1, ((8 - s) % 8) * 16 : ((8 - s) % 8) * 16 + 16] for s in range(8)], axis=0
        )

    peaks, totals, teachers = gathered(0), gathered(1), gathered(2)
    peak = jnp.max(peaks, axis=0, keepdims=True)
    total = jnp.sum(totals * jnp.exp(peaks - peak), axis=0, keepdims=True)
    lse = peak + jnp.log(total)
    loss_ref[...] = entropy_lanes - jnp.sum(teachers, axis=0, keepdims=True) + lse
    share = jnp.exp(peaks - lse)
    row = iota((16, 16), 0)
    own_lane = iota((16, 16), 1) == slab * 2 + (row & 1)
    columns = [
        jnp.sum(jnp.where(own_lane, share[s : s + 1, :], 0.0), axis=1, keepdims=True) for s in range(8)
    ]
    for copy in z_copies:
        copy.wait_recv()
    z_in[0] = z_out[0]
    result = None
    for s in range(8):
        block = z_in[s].astype(F32)
        term = block[0:12] * columns[s][0:12] - block[12:24]
        result = term if result is None else result + term
    result = scale * result
    for b in range(6):
        grad_ref[:, b * 128 : (b + 1) * 128] = result[2 * b : 2 * b + 2]

    swap.wait_send()
    for copy in sent:
        copy.wait_send()


def shards(queries, teacher_weight, cand_ids, passages):
    rows, depth = queries.shape
    width = passages.shape[0]
    num_cand = cand_ids.shape[1]
    stride = width * 256 // num_cand
    scale = 3.0 / math.sqrt(depth)
    vmem = pl.BlockSpec(memory_space=pltpu.VMEM)
    dma = pltpu.SemaphoreType.DMA
    loss, grad = pl.pallas_call(
        functools.partial(kernel, stride, scale),
        out_shape=(jax.ShapeDtypeStruct((1, rows), F32), jax.ShapeDtypeStruct((2, depth), F32)),
        in_specs=[vmem, vmem, vmem, pl.BlockSpec(memory_space=pl.ANY)],
        out_specs=(vmem, vmem),
        scratch_shapes=[
            pltpu.VMEM((2, width, depth), BF16),
            pltpu.VMEM((16, 16, depth), BF16),
            pltpu.VMEM((16, 16, 128), BF16),
            pltpu.VMEM((8, 16, 128), BF16),
            pltpu.VMEM((256, 256), BF16),
            pltpu.VMEM((16, 16, depth), BF16),
            pltpu.VMEM((16, 16, depth), BF16),
            pltpu.VMEM((2, 8, 128), F32),
            pltpu.VMEM((16, 16, depth), BF16),
            pltpu.VMEM((16, 16, depth), BF16),
            pltpu.VMEM((16, 8, 128), F32),
            pltpu.VMEM((8, 32, 128), BF16),
            pltpu.VMEM((8, 32, 128), BF16),
            pltpu.VMEM((8, 128), F32),
            pltpu.VMEM((8, 8, 128), F32),
            dma((3,)),
            dma((2, 15)),
            dma((2, 15)),
            dma((2, 15)),
            dma((2, 15)),
            dma((2, 15)),
            dma((2, 7)),
            dma((2, 7)),
        ],
        compiler_params=pltpu.CompilerParams(
            collective_id=0, has_side_effects=True, vmem_limit_bytes=48 * 1024 * 1024
        ),
    )(queries, teacher_weight, cand_ids, passages)
    return (loss.reshape(rows), grad)


def solution(mesh):
    return jax.shard_map(
        shards,
        mesh=mesh,
        in_specs=(P("blk", None), P("blk", None), P("blk", None), P(("blk", "slab"), None)),
        out_specs=(P("blk"), P(("blk", "slab"), None)),
        check_vma=False,
    )
```

```python
import functools
import math

import jax
import jax.numpy as jnp
from jax import lax
from jax.experimental import pallas as pl
from jax.experimental.pallas import tpu as pltpu
from jax.sharding import PartitionSpec as P

MESH = pl.DeviceIdType.MESH
F32 = jnp.float32
BF16 = jnp.bfloat16
I32 = jnp.int32
FAR_FIRST = (4, 3, 5, 2, 6, 1, 7, 0)


def position():
    blk = lax.axis_index("blk")
    slab = lax.axis_index("slab")
    z = blk // 4
    y = ((blk // 2) % 2) * 2 + slab % 2
    return slab // 2, y, z, blk % 2


def device(x, y, z, core):
    return {"blk": (z * 2 + y // 2) * 2 + core, "slab": x * 2 + y % 2}


def iota(shape, dim):
    return lax.broadcasted_iota(I32, shape, dim)


def split3(value):
    first = value.astype(BF16)
    rest = value - first.astype(F32)
    second = rest.astype(BF16)
    third = (rest - second.astype(F32)).astype(BF16)
    return first, second, third


def kernel(
    stride,
    scale,
    q_hbm,
    w_hbm,
    id_hbm,
    pas_ref,
    loss_ref,
    grad_ref,
    q_ref,
    w_ref,
    id_ref,
    pas,
    queries,
    cands,
    cand_out,
    perm_ref,
    prob_out,
    exp_out,
    stat_out,
    prob_in,
    exp_in,
    stat_in,
    z_out,
    z_in,
    zstat_out,
    zstat_in,
    in_sems,
    pas_sem,
    q_sems,
    c_sems,
    prob_sems,
    exp_sems,
    stat_sems,
    z_sems,
    zstat_sems,
):
    x, y, z, core = position()
    y_hi, y_lo = y // 2, y % 2
    slab = x * 2 + y_lo
    width = pas_ref.shape[0]
    num_cand = id_ref.shape[1]
    plane = width * 32
    per_plane = plane // stride

    gather_to = [
        (device(x, y if dy == 0 else 3 - y, (z + d) % 8, core), dy * 8 + (8 - d) % 8, d)
        for d in FAR_FIRST
        for dy in (0, 1)
        if (d, dy) != (0, 0)
    ]
    plane_to = [
        (
            device((x + ex) % 4, (y + ey) % 4, z, core),
            ex * 4 + ey,
            ((4 - ex) % 4) * 4 + (4 - ey) % 4,
            (((y + ey) % 4) // 2 + y_hi) % 2,
        )
        for ex in (2, 1, 3, 0)
        for ey in (2, 1, 3, 0)
        if (ex, ey) != (0, 0)
    ]
    z_to = [(device(x, y, (z + d) % 8, core), d, (8 - d) % 8) for d in FAR_FIRST if d]
    other = device(x, y, z, 1 - core)

    barrier = pltpu.get_barrier_semaphore()
    greeted = [other] + [p[0] for p in plane_to]
    greeted += [p[0] for p in gather_to if p[2] != 0]
    for target in greeted:
        pl.semaphore_signal(barrier, inc=1, device_id=target, device_id_type=MESH)

    small = [
        pltpu.make_async_copy(src, dst, in_sems.at[i])
        for i, (src, dst) in enumerate(((w_hbm, w_ref), (id_hbm, id_ref), (q_hbm, q_ref)))
    ]
    for copy in small:
        copy.start()
    load = pltpu.make_async_copy(pas_ref, pas.at[0], pas_sem.at[0])
    load.start()
    for copy in small:
        copy.wait()

    weights = w_ref[...].astype(F32)
    weight_sum = jnp.sum(weights, axis=1, keepdims=True)
    own_prob = weights / weight_sum
    entropy = jnp.sum(own_prob * jnp.log(own_prob), axis=1, keepdims=True)
    pad = 256 - num_cand
    wide_w = jnp.concatenate([weights, jnp.zeros((16, pad), F32)], axis=1)
    wide_id = jnp.concatenate([id_ref[...], jnp.zeros((16, pad), I32)], axis=1)
    s1, s2, s3 = split3(weight_sum)
    lane32 = iota((16, 32), 1)
    sums = jnp.where(
        lane32 == 0,
        s1.astype(F32),
        jnp.where(lane32 == 1, s2.astype(F32), jnp.where(lane32 == 2, s3.astype(F32), 0.0)),
    )
    for zz in range(8):
        lo = per_plane * zz
        ids = jnp.maximum(wide_id[:, lo : lo + 32] - lo * stride, 0)
        high = (ids >> 8).astype(F32)
        low = (ids & 255).astype(F32)
        cand_out[zz] = jnp.concatenate([high, low, wide_w[:, lo : lo + 32], sums], axis=1).astype(BF16)
    cands[0] = cand_out[z]
    queries[0] = q_ref[...]

    p_row = iota((256, 1), 0)
    p_x = (x + (p_row >> 6)) & 3
    p_y = (y + ((p_row >> 4) & 3)) & 3
    p_dy = ((p_y >> 1) + y_hi) & 1
    p_n = p_dy * 128 + ((p_row >> 1) & 7) * 16 + (p_x * 2 + (p_y & 1)) * 2 + (p_row & 1)
    hot = (iota((256, 256), 1) == p_n).astype(F32)
    perm_ref[...] = hot.astype(BF16)

    pl.semaphore_wait(barrier, len(greeted))

    swap = pltpu.make_async_remote_copy(
        pas_ref, pas.at[1], pas_sem.at[1], pas_sem.at[2], device_id=other, device_id_type=MESH
    )
    swap.start()
    sent = []
    cand_copies, q_copies = {}, {}
    for i, (target, slot, d) in enumerate(gather_to):
        copy = pltpu.make_async_remote_copy(
            cand_out.at[(z + d) % 8],
            cands.at[slot],
            c_sems.at[0, i],
            c_sems.at[1, i],
            device_id=target,
            device_id_type=MESH,
        )
        copy.start()
        cand_copies[i] = copy
    for i, (target, slot, d) in enumerate(gather_to):
        copy = pltpu.make_async_remote_copy(
            q_ref,
            queries.at[slot],
            q_sems.at[0, i],
            q_sems.at[1, i],
            device_id=target,
            device_id_type=MESH,
        )
        copy.start()
        q_copies[i] = copy
    sent += list(cand_copies.values()) + list(q_copies.values())

    offsets = [((((z * 2 + y_hi) * 2 + c) * 8) + slab) * width for c in (core, 1 - core)]
    firsts = [jnp.minimum(off // stride, num_cand - 2) - per_plane * z for off in offsets]
    out_lane = iota((1, 128), 1)
    target_lane = jnp.where((out_lane >= 12) & (out_lane < 15), 96 + out_lane - 12, -1)
    for rho in range(2):
        for c in range(2):
            for field in range(3):
                target_lane = jnp.where(
                    out_lane == (rho * 2 + c) * 3 + field, field * 32 + firsts[rho] + c, target_lane
                )
    pick = (iota((128, 128), 0) == target_lane).astype(F32).astype(BF16)
    for copy in cand_copies.values():
        copy.wait_recv()
    picked = jnp.dot(cands[...].reshape(256, 128), pick, preferred_element_type=F32).astype(BF16)
    picked = jnp.dot(perm_ref[...], picked, preferred_element_type=F32)
    total_w = picked[:, 12:13] + picked[:, 13:14] + picked[:, 14:15]
    load.wait()
    column = iota((256, width), 1).astype(F32)
    prob_sum = None
    swap.wait_recv()
    for rho in range(2):
        shift = (per_plane * stride * z - offsets[rho]).astype(F32)
        dense = None
        for c in range(2):
            at = (rho * 2 + c) * 3
            local = picked[:, at : at + 1] * 256.0 + picked[:, at + 1 : at + 2] + shift
            prob = picked[:, at + 2 : at + 3] / total_w
            term = jnp.where(column == local, prob, 0.0)
            dense = term if dense is None else dense + term
        part = jnp.dot(dense.astype(BF16), pas[rho], preferred_element_type=F32)
        prob_sum = part if prob_sum is None else prob_sum + part
    prob_out[...] = prob_sum.astype(BF16).reshape(16, 16, -1)
    prob_copies = []
    for i, (target, group, slot, _) in enumerate(plane_to):
        copy = pltpu.make_async_remote_copy(
            prob_out.at[group],
            prob_in.at[slot],
            prob_sems.at[0, i],
            prob_sems.at[1, i],
            device_id=target,
            device_id_type=MESH,
        )
        copy.start()
        prob_copies.append(copy)
    sent += prob_copies

    for copy in q_copies.values():
        copy.wait_recv()
    depth = q_ref.shape[1]
    rows = jnp.dot(perm_ref[...], queries[...].reshape(256, depth), preferred_element_type=F32)
    rows16 = rows.astype(BF16)
    teacher = scale * jnp.sum(rows * prob_sum, axis=1, keepdims=True)
    nt = (((1,), (1,)), ((), ()))
    scores = [
        scale * lax.dot_general(rows16, pas[rho], nt, preferred_element_type=F32) for rho in range(2)
    ]
    peak = jnp.maximum(
        jnp.max(scores[0], axis=1, keepdims=True), jnp.max(scores[1], axis=1, keepdims=True)
    )
    exps = [jnp.exp(s - peak) for s in scores]
    total = jnp.sum(exps[0], axis=1, keepdims=True) + jnp.sum(exps[1], axis=1, keepdims=True)
    mixed = jnp.dot(exps[0].astype(BF16), pas[0], preferred_element_type=F32) + jnp.dot(
        exps[1].astype(BF16), pas[1], preferred_element_type=F32
    )
    exp_out[...] = mixed.astype(BF16).reshape(16, 16, depth)
    mask = perm_ref[...].astype(F32) > 0.5
    for k, stat in enumerate((peak, total, teacher)):
        lanes = jnp.sum(jnp.where(mask, stat, 0.0), axis=0, keepdims=True)
        stat_out[0, k : k + 1, :] = lanes[:, :128]
        stat_out[1, k : k + 1, :] = lanes[:, 128:]
    exp_copies, stat_copies = [], []
    for i, (target, group, slot, dy) in enumerate(plane_to):
        copy = pltpu.make_async_remote_copy(
            stat_out.at[dy],
            stat_in.at[slot],
            stat_sems.at[0, i],
            stat_sems.at[1, i],
            device_id=target,
            device_id_type=MESH,
        )
        copy.start()
        stat_copies.append(copy)
        copy = pltpu.make_async_remote_copy(
            exp_out.at[group],
            exp_in.at[slot],
            exp_sems.at[0, i],
            exp_sems.at[1, i],
            device_id=target,
            device_id_type=MESH,
        )
        copy.start()
        exp_copies.append(copy)
    sent += exp_copies + stat_copies

    stat_in[0] = stat_out[0]
    for copy in prob_copies:
        copy.wait_recv()
    prob_rows = prob_out[0].astype(F32)
    for i in range(1, 16):
        prob_rows = prob_rows + prob_in[i].astype(F32)
    for copy in stat_copies:
        copy.wait_recv()
    peaks = jnp.concatenate([stat_in[i, 0:1, :] for i in range(16)], axis=0)
    totals = jnp.concatenate([stat_in[i, 1:2, :] for i in range(16)], axis=0)
    teachers = jnp.concatenate([stat_in[i, 2:3, :] for i in range(16)], axis=0)
    peak = jnp.max(peaks, axis=0, keepdims=True)
    share = jnp.exp(peaks - peak)
    total = jnp.sum(totals * share, axis=0, keepdims=True)
    teacher = jnp.sum(teachers, axis=0, keepdims=True)
    zstat_out[0:1, :] = peak
    zstat_out[1:2, :] = total
    zstat_out[2:3, :] = teacher
    zstat_copies = []
    for i, (target, d, slot) in enumerate(z_to):
        copy = pltpu.make_async_remote_copy(
            zstat_out,
            zstat_in.at[slot],
            zstat_sems.at[0, i],
            zstat_sems.at[1, i],
            device_id=target,
            device_id_type=MESH,
        )
        copy.start()
        zstat_copies.append(copy)
    row = iota((16, 128), 0)
    own_lane = iota((16, 128), 1) == (row >> 1) * 16 + slab * 2 + (row & 1)
    columns = [
        jnp.sum(jnp.where(own_lane, share[i : i + 1, :], 0.0), axis=1, keepdims=True) for i in range(16)
    ]
    for copy in exp_copies:
        copy.wait_recv()
    exp_rows = exp_out[0].astype(F32) * columns[0]
    for i in range(1, 16):
        exp_rows = exp_rows + exp_in[i].astype(F32) * columns[i]

    stacked = jnp.concatenate(
        [part[:, b * 128 : (b + 1) * 128] for part in (exp_rows, prob_rows) for b in range(6)], axis=0
    )
    coarse = stacked.astype(BF16)
    fine = (stacked - coarse.astype(F32)).astype(BF16)
    stacked = jnp.concatenate([coarse, fine], axis=0)
    o = iota((384, 1), 0)
    d_of = o // 48
    j = o - 48 * d_of
    part = j // 12
    jj = j - 12 * part
    source = part * 96 + (jj >> 1) * 16 + d_of * 2 + (jj & 1)
    order = (iota((384, 384), 1) == source).astype(F32).astype(BF16)
    z_out[...] = jnp.dot(order, stacked, preferred_element_type=F32).astype(BF16).reshape(8, 48, 128)
    z_copies = []
    for i, (target, d, slot) in enumerate(z_to):
        copy = pltpu.make_async_remote_copy(
            z_out.at[d],
            z_in.at[slot],
            z_sems.at[0, i],
            z_sems.at[1, i],
            device_id=target,
            device_id_type=MESH,
        )
        copy.start()
        z_copies.append(copy)
    sent += zstat_copies + z_copies

    zstat_in[0] = zstat_out[...]
    entropy_lanes = jnp.sum(
        jnp.where(iota((16, 16), 0) == iota((16, 16), 1), entropy, 0.0), axis=0, keepdims=True
    )
    for copy in zstat_copies:
        copy.wait_recv()

    def gathered(k):
        return jnp.concatenate(
            [zstat_in[s, k : k + 1, ((8 - s) % 8) * 16 : ((8 - s) % 8) * 16 + 16] for s in range(8)], axis=0
        )

    peaks, totals, teachers = gathered(0), gathered(1), gathered(2)
    peak = jnp.max(peaks, axis=0, keepdims=True)
    total = jnp.sum(totals * jnp.exp(peaks - peak), axis=0, keepdims=True)
    lse = peak + jnp.log(total)
    loss_ref[...] = entropy_lanes - jnp.sum(teachers, axis=0, keepdims=True) + lse
    share = jnp.exp(peaks - lse)
    row = iota((16, 16), 0)
    own_lane = iota((16, 16), 1) == slab * 2 + (row & 1)
    columns = [
        jnp.sum(jnp.where(own_lane, share[s : s + 1, :], 0.0), axis=1, keepdims=True) for s in range(8)
    ]
    for copy in z_copies:
        copy.wait_recv()
    z_in[0] = z_out[0]
    result = None
    for s in range(8):
        block = z_in[s].astype(F32)
        block = block[0:24] + block[24:48]
        term = block[0:12] * columns[s][0:12] - block[12:24]
        result = term if result is None else result + term
    result = scale * result
    for b in range(6):
        grad_ref[:, b * 128 : (b + 1) * 128] = result[2 * b : 2 * b + 2]

    swap.wait_send()
    for copy in sent:
        copy.wait_send()


def shards(queries, teacher_weight, cand_ids, passages):
    rows, depth = queries.shape
    width = passages.shape[0]
    num_cand = cand_ids.shape[1]
    stride = width * 256 // num_cand
    scale = 3.0 / math.sqrt(depth)
    vmem = pl.BlockSpec(memory_space=pltpu.VMEM)
    dma = pltpu.SemaphoreType.DMA
    loss, grad = pl.pallas_call(
        functools.partial(kernel, stride, scale),
        out_shape=(pltpu.VMEM((1, rows), F32), pltpu.VMEM((2, depth), F32)),
        in_specs=[pl.BlockSpec(memory_space=pltpu.HBM)] * 4,
        out_specs=(vmem, vmem),
        scratch_shapes=[
            pltpu.VMEM((rows, depth), BF16),
            pltpu.VMEM((rows, num_cand), BF16),
            pltpu.VMEM((rows, num_cand), I32),
            pltpu.VMEM((2, width, depth), BF16),
            pltpu.VMEM((16, 16, depth), BF16),
            pltpu.VMEM((16, 16, 128), BF16),
            pltpu.VMEM((8, 16, 128), BF16),
            pltpu.VMEM((256, 256), BF16),
            pltpu.VMEM((16, 16, depth), BF16),
            pltpu.VMEM((16, 16, depth), BF16),
            pltpu.VMEM((2, 8, 128), F32),
            pltpu.VMEM((16, 16, depth), BF16),
            pltpu.VMEM((16, 16, depth), BF16),
            pltpu.VMEM((16, 8, 128), F32),
            pltpu.VMEM((8, 48, 128), BF16),
            pltpu.VMEM((8, 48, 128), BF16),
            pltpu.VMEM((8, 128), F32),
            pltpu.VMEM((8, 8, 128), F32),
            dma((3,)),
            dma((3,)),
            dma((2, 15)),
            dma((2, 15)),
            dma((2, 15)),
            dma((2, 15)),
            dma((2, 15)),
            dma((2, 7)),
            dma((2, 7)),
        ],
        compiler_params=pltpu.CompilerParams(
            collective_id=0, has_side_effects=True, vmem_limit_bytes=60 * 1024 * 1024
        ),
    )(*(pltpu.with_memory_space_constraint(a, pltpu.HBM) for a in (queries, teacher_weight, cand_ids, passages)))
    return (loss.reshape(rows), grad)


def solution(mesh):
    return jax.shard_map(
        shards,
        mesh=mesh,
        in_specs=(P("blk", None), P("blk", None), P("blk", None), P(("blk", "slab"), None)),
        out_specs=(P("blk"), P(("blk", "slab"), None)),
        check_vma=False,
    )
```

```python
import functools
import math

import jax
import jax.numpy as jnp
from jax import lax
from jax.experimental import pallas as pl
from jax.experimental.pallas import tpu as pltpu
from jax.sharding import PartitionSpec as P

MESH = pl.DeviceIdType.MESH
F32 = jnp.float32
BF16 = jnp.bfloat16
I32 = jnp.int32
FAR_FIRST = (4, 3, 5, 2, 6, 1, 7)
RELAYED = (1, 7, 2, 6)
DIRECT = (4, 3, 5)


def position():
    blk = lax.axis_index("blk")
    slab = lax.axis_index("slab")
    z = blk // 4
    y = ((blk // 2) % 2) * 2 + slab % 2
    return slab // 2, y, z, blk % 2


def device(x, y, z, core):
    return {"blk": (z * 2 + y // 2) * 2 + core, "slab": x * 2 + y % 2}


def iota(shape, dim):
    return lax.broadcasted_iota(I32, shape, dim)


def split3(value):
    first = value.astype(BF16)
    rest = value - first.astype(F32)
    second = rest.astype(BF16)
    third = (rest - second.astype(F32)).astype(BF16)
    return first, second, third


def kernel(
    stride,
    scale,
    q_hbm,
    w_hbm,
    id_hbm,
    pas_ref,
    loss_ref,
    grad_ref,
    q_ref,
    w_ref,
    id_ref,
    pas,
    queries,
    cands,
    cand_out,
    perm_ref,
    prob_out,
    exp_out,
    stat_out,
    prob_in,
    exp_in,
    stat_in,
    z_out,
    z_in,
    zstat_out,
    zstat_in,
    in_sems,
    pas_sem,
    q_sems,
    c_sems,
    prob_sems,
    exp_sems,
    stat_sems,
    z_sems,
    zstat_sems,
):
    x, y, z, core = position()
    y_hi, y_lo = y // 2, y % 2
    slab = x * 2 + y_lo
    width = pas_ref.shape[0]
    num_cand = id_ref.shape[1]
    plane = width * 32
    per_plane = plane // stride

    plane_to = [
        (
            device((x + ex) % 4, ((y_hi + dy) % 2) * 2 + (y_lo + eyl) % 2, z, core),
            dy * 8 + ex * 2 + eyl,
            dy * 8 + ((4 - ex) % 4) * 2 + eyl,
        )
        for dy in (0, 1)
        for ex in (2, 1, 3, 0)
        for eyl in (0, 1)
        if (dy, ex, eyl) != (0, 0, 0)
    ]
    z_to = [(device(x, y, (z + d) % 8, core), d, (8 - d) % 8) for d in FAR_FIRST]
    other = device(x, y, z, 1 - core)

    barrier = pltpu.get_barrier_semaphore()
    greeted = [p[0] for p in plane_to] + [other]
    greeted = [device(x, 3 - y, (z + d) % 8, core) for d in FAR_FIRST] + greeted
    greeted = [p[0] for p in z_to] + greeted
    for target in greeted:
        pl.semaphore_signal(barrier, inc=1, device_id=target, device_id_type=MESH)

    small = [
        pltpu.make_async_copy(src, dst, in_sems.at[i])
        for i, (src, dst) in enumerate(((w_hbm, w_ref), (id_hbm, id_ref), (q_hbm, q_ref)))
    ]
    for copy in small:
        copy.start()
    load = pltpu.make_async_copy(pas_ref, pas.at[0], pas_sem.at[0])
    load.start()
    for copy in small:
        copy.wait()

    weights = w_ref[...].astype(F32)
    weight_sum = jnp.sum(weights, axis=1, keepdims=True)
    own_prob = weights / weight_sum
    entropy = jnp.sum(own_prob * jnp.log(own_prob), axis=1, keepdims=True)
    pad = 256 - num_cand
    wide_w = jnp.concatenate([weights, jnp.zeros((16, pad), F32)], axis=1)
    wide_id = jnp.concatenate([id_ref[...], jnp.zeros((16, pad), I32)], axis=1)
    s1, s2, s3 = split3(weight_sum)
    lane32 = iota((16, 32), 1)
    sums = jnp.where(
        lane32 == 0,
        s1.astype(F32),
        jnp.where(lane32 == 1, s2.astype(F32), jnp.where(lane32 == 2, s3.astype(F32), 0.0)),
    )
    for zz in range(8):
        lo = per_plane * zz
        ids = jnp.maximum(wide_id[:, lo : lo + 32] - lo * stride, 0)
        high = (ids >> 8).astype(F32)
        low = (ids & 255).astype(F32)
        cand_out[zz] = jnp.concatenate([high, low, wide_w[:, lo : lo + 32], sums], axis=1).astype(BF16)
    cands[0] = cand_out[z]
    queries[0] = q_ref[...]

    p_row = iota((128, 1), 0)
    p_x = (x + (p_row >> 5)) & 3
    p_y = (y_lo + ((p_row >> 4) & 1)) & 1
    p_n = ((p_row >> 1) & 7) * 16 + (p_x * 2 + p_y) * 2 + (p_row & 1)
    mask = iota((128, 128), 1) == p_n
    perm_ref[...] = mask.astype(F32).astype(BF16)

    pl.semaphore_wait(barrier, len(greeted))

    swap = pltpu.make_async_remote_copy(
        pas_ref, pas.at[1], pas_sem.at[1], pas_sem.at[2], device_id=other, device_id_type=MESH
    )
    swap.start()
    sent = []
    mirror = device(x, 3 - y, z, core)

    def send(src, dst, sems, i, target):
        copy = pltpu.make_async_remote_copy(
            src, dst, sems.at[0, i], sems.at[1, i], device_id=target, device_id_type=MESH
        )
        copy.start()
        sent.append(copy)
        return copy

    cand_copies, near_copies, low_copies, high_copies = [], {}, [], []
    for d in FAR_FIRST + (0,):
        for dy in (0, 1):
            if d or dy:
                target = device(x, 3 - y if dy else y, (z + d) % 8, core)
                slot = dy * 8 + (8 - d) % 8
                cand_copies.append(send(cand_out.at[(z + d) % 8], cands.at[slot], c_sems, slot, target))
    for d in RELAYED:
        target = device(x, y, (z + d) % 8, core)
        near_copies[d] = send(q_ref, queries.at[8 - d], q_sems, d, target)
    for d in DIRECT:
        target = device(x, y, (z + d) % 8, core)
        low_copies.append(send(q_ref, queries.at[8 - d], q_sems, d, target))
    for d in DIRECT:
        target = device(x, 3 - y, (z + d) % 8, core)
        high_copies.append(send(q_ref, queries.at[16 - d], q_sems, 8 + d, target))
    high_copies.append(send(q_ref, queries.at[8], q_sems, 8, mirror))
    for d in RELAYED:
        near_copies[d].wait_recv()
        high_copies.append(send(queries.at[8 - d], queries.at[16 - d], q_sems, 8 + d, mirror))

    offsets = [((((z * 2 + y_hi) * 2 + c) * 8) + slab) * width for c in (core, 1 - core)]
    firsts = [jnp.minimum(off // stride, num_cand - 2) - per_plane * z for off in offsets]
    out_lane = iota((1, 128), 1)
    target_lane = jnp.where((out_lane >= 12) & (out_lane < 15), 96 + out_lane - 12, -1)
    for rho in range(2):
        for c in range(2):
            for field in range(3):
                target_lane = jnp.where(
                    out_lane == (rho * 2 + c) * 3 + field, field * 32 + firsts[rho] + c, target_lane
                )
    pick = (iota((128, 128), 0) == target_lane).astype(F32).astype(BF16)
    for copy in cand_copies:
        copy.wait_recv()
    picked = jnp.dot(cands[...].reshape(256, 128), pick, preferred_element_type=F32).astype(BF16)
    picked = jnp.concatenate(
        [
            jnp.dot(perm_ref[...], picked[h * 128 : h * 128 + 128], preferred_element_type=F32)
            for h in range(2)
        ],
        axis=0,
    )
    total_w = picked[:, 12:13] + picked[:, 13:14] + picked[:, 14:15]
    load.wait()
    column = iota((256, width), 1).astype(F32)
    prob_sum = None
    swap.wait_recv()
    for rho in range(2):
        shift = (per_plane * stride * z - offsets[rho]).astype(F32)
        dense = None
        for c in range(2):
            at = (rho * 2 + c) * 3
            local = picked[:, at : at + 1] * 256.0 + picked[:, at + 1 : at + 2] + shift
            prob = picked[:, at + 2 : at + 3] / total_w
            term = jnp.where(column == local, prob, 0.0)
            dense = term if dense is None else dense + term
        part = jnp.dot(dense.astype(BF16), pas[rho], preferred_element_type=F32)
        prob_sum = part if prob_sum is None else prob_sum + part
    prob_out[...] = prob_sum.astype(BF16).reshape(16, 16, -1)
    prob_copies = [
        send(prob_out.at[group], prob_in.at[slot], prob_sems, i, target)
        for i, (target, group, slot) in enumerate(plane_to)
    ]

    depth = q_ref.shape[1]
    nt = (((1,), (1,)), ((), ()))
    exp_copies, stat_copies = [], []
    for h, waits in enumerate((low_copies, high_copies)):
        for copy in waits:
            copy.wait_recv()
        half = queries[h * 8 : h * 8 + 8].reshape(128, depth)
        rows = jnp.dot(perm_ref[...], half, preferred_element_type=F32)
        rows16 = rows.astype(BF16)
        scores = [
            scale * lax.dot_general(rows16, pas[rho], nt, preferred_element_type=F32)
            for rho in range(2)
        ]
        peak = jnp.maximum(
            jnp.max(scores[0], axis=1, keepdims=True), jnp.max(scores[1], axis=1, keepdims=True)
        )
        exps = [jnp.exp(s - peak) for s in scores]
        mixed = jnp.dot(exps[0].astype(BF16), pas[0], preferred_element_type=F32) + jnp.dot(
            exps[1].astype(BF16), pas[1], preferred_element_type=F32
        )
        exp_out[h * 8 : h * 8 + 8] = mixed.astype(BF16).reshape(8, 16, depth)
        for i, (target, group, slot) in enumerate(plane_to):
            if group // 8 == h:
                exp_copies.append(send(exp_out.at[group], exp_in.at[slot], exp_sems, i, target))
        total = jnp.sum(exps[0], axis=1, keepdims=True) + jnp.sum(exps[1], axis=1, keepdims=True)
        teacher = scale * jnp.sum(rows * prob_sum[h * 128 : h * 128 + 128], axis=1, keepdims=True)
        for k, stat in enumerate((peak, total, teacher)):
            stat_out[h, k : k + 1, :] = jnp.sum(jnp.where(mask, stat, 0.0), axis=0, keepdims=True)
        for i, (target, group, slot) in enumerate(plane_to):
            if group // 8 == h:
                stat_copies.append(send(stat_out.at[h], stat_in.at[slot], stat_sems, i, target))

    stat_in[0] = stat_out[0]
    for copy in prob_copies:
        copy.wait_recv()
    prob_rows = prob_out[0].astype(F32)
    for i in range(1, 16):
        prob_rows = prob_rows + prob_in[i].astype(F32)
    for copy in stat_copies:
        copy.wait_recv()
    peaks = jnp.concatenate([stat_in[i, 0:1, :] for i in range(16)], axis=0)
    totals = jnp.concatenate([stat_in[i, 1:2, :] for i in range(16)], axis=0)
    teachers = jnp.concatenate([stat_in[i, 2:3, :] for i in range(16)], axis=0)
    peak = jnp.max(peaks, axis=0, keepdims=True)
    share = jnp.exp(peaks - peak)
    total = jnp.sum(totals * share, axis=0, keepdims=True)
    teacher = jnp.sum(teachers, axis=0, keepdims=True)
    zstat_out[0:1, :] = peak
    zstat_out[1:2, :] = total
    zstat_out[2:3, :] = teacher
    zstat_copies = [
        send(zstat_out, zstat_in.at[slot], zstat_sems, i, target)
        for i, (target, d, slot) in enumerate(z_to)
    ]
    row = iota((16, 128), 0)
    own_lane = iota((16, 128), 1) == (row >> 1) * 16 + slab * 2 + (row & 1)
    columns = [
        jnp.sum(jnp.where(own_lane, share[i : i + 1, :], 0.0), axis=1, keepdims=True) for i in range(16)
    ]
    for copy in exp_copies:
        copy.wait_recv()
    exp_rows = exp_out[0].astype(F32) * columns[0]
    for i in range(1, 16):
        exp_rows = exp_rows + exp_in[i].astype(F32) * columns[i]

    stacked = jnp.concatenate(
        [part[:, b * 128 : (b + 1) * 128] for part in (exp_rows, prob_rows) for b in range(6)], axis=0
    )
    coarse = stacked.astype(BF16)
    fine = (stacked - coarse.astype(F32)).astype(BF16)
    stacked = jnp.concatenate([coarse, fine], axis=0)
    o = iota((384, 1), 0)
    d_of = o // 48
    j = o - 48 * d_of
    part = j // 12
    jj = j - 12 * part
    source = part * 96 + (jj >> 1) * 16 + d_of * 2 + (jj & 1)
    order = (iota((384, 384), 1) == source).astype(F32).astype(BF16)
    z_out[...] = jnp.dot(order, stacked, preferred_element_type=F32).astype(BF16).reshape(8, 48, 128)
    z_copies = [
        send(z_out.at[d], z_in.at[slot], z_sems, i, target) for i, (target, d, slot) in enumerate(z_to)
    ]

    zstat_in[0] = zstat_out[...]
    entropy_lanes = jnp.sum(
        jnp.where(iota((16, 16), 0) == iota((16, 16), 1), entropy, 0.0), axis=0, keepdims=True
    )
    for copy in zstat_copies:
        copy.wait_recv()

    def gathered(k):
        return jnp.concatenate(
            [zstat_in[s, k : k + 1, ((8 - s) % 8) * 16 : ((8 - s) % 8) * 16 + 16] for s in range(8)], axis=0
        )

    peaks, totals, teachers = gathered(0), gathered(1), gathered(2)
    peak = jnp.max(peaks, axis=0, keepdims=True)
    total = jnp.sum(totals * jnp.exp(peaks - peak), axis=0, keepdims=True)
    lse = peak + jnp.log(total)
    loss_ref[...] = entropy_lanes - jnp.sum(teachers, axis=0, keepdims=True) + lse
    share = jnp.exp(peaks - lse)
    row = iota((16, 16), 0)
    own_lane = iota((16, 16), 1) == slab * 2 + (row & 1)
    columns = [
        jnp.sum(jnp.where(own_lane, share[s : s + 1, :], 0.0), axis=1, keepdims=True) for s in range(8)
    ]
    for copy in z_copies:
        copy.wait_recv()
    z_in[0] = z_out[0]
    result = None
    for s in range(8):
        block = z_in[s].astype(F32)
        block = block[0:24] + block[24:48]
        term = block[0:12] * columns[s][0:12] - block[12:24]
        result = term if result is None else result + term
    result = scale * result
    for b in range(6):
        grad_ref[:, b * 128 : (b + 1) * 128] = result[2 * b : 2 * b + 2]

    swap.wait_send()
    for copy in sent:
        copy.wait_send()


def shards(queries, teacher_weight, cand_ids, passages):
    rows, depth = queries.shape
    width = passages.shape[0]
    num_cand = cand_ids.shape[1]
    stride = width * 256 // num_cand
    scale = 3.0 / math.sqrt(depth)
    vmem = pl.BlockSpec(memory_space=pltpu.VMEM)
    dma = pltpu.SemaphoreType.DMA
    loss, grad = pl.pallas_call(
        functools.partial(kernel, stride, scale),
        out_shape=(pltpu.VMEM((1, rows), F32), pltpu.VMEM((2, depth), F32)),
        in_specs=[pl.BlockSpec(memory_space=pltpu.HBM)] * 4,
        out_specs=(vmem, vmem),
        scratch_shapes=[
            pltpu.VMEM((rows, depth), BF16),
            pltpu.VMEM((rows, num_cand), BF16),
            pltpu.VMEM((rows, num_cand), I32),
            pltpu.VMEM((2, width, depth), BF16),
            pltpu.VMEM((16, 16, depth), BF16),
            pltpu.VMEM((16, 16, 128), BF16),
            pltpu.VMEM((8, 16, 128), BF16),
            pltpu.VMEM((128, 128), BF16),
            pltpu.VMEM((16, 16, depth), BF16),
            pltpu.VMEM((16, 16, depth), BF16),
            pltpu.VMEM((2, 8, 128), F32),
            pltpu.VMEM((16, 16, depth), BF16),
            pltpu.VMEM((16, 16, depth), BF16),
            pltpu.VMEM((16, 8, 128), F32),
            pltpu.VMEM((8, 48, 128), BF16),
            pltpu.VMEM((8, 48, 128), BF16),
            pltpu.VMEM((8, 128), F32),
            pltpu.VMEM((8, 8, 128), F32),
            dma((3,)),
            dma((3,)),
            dma((2, 16)),
            dma((2, 16)),
            dma((2, 15)),
            dma((2, 15)),
            dma((2, 15)),
            dma((2, 7)),
            dma((2, 7)),
        ],
        compiler_params=pltpu.CompilerParams(
            collective_id=0, has_side_effects=True, vmem_limit_bytes=60 * 1024 * 1024
        ),
    )(*(pltpu.with_memory_space_constraint(a, pltpu.HBM) for a in (queries, teacher_weight, cand_ids, passages)))
    return (loss.reshape(rows), grad)


def solution(mesh):
    return jax.shard_map(
        shards,
        mesh=mesh,
        in_specs=(P("blk", None), P("blk", None), P("blk", None), P(("blk", "slab"), None)),
        out_specs=(P("blk"), P(("blk", "slab"), None)),
        check_vma=False,
    )
```

```python
import functools
import math

import jax
import jax.numpy as jnp
from jax import lax
from jax.experimental import pallas as pl
from jax.experimental.pallas import tpu as pltpu
from jax.sharding import PartitionSpec as P

MESH = pl.DeviceIdType.MESH
F32 = jnp.float32
BF16 = jnp.bfloat16
I32 = jnp.int32
FAR_FIRST = (4, 3, 5, 2, 6, 1, 7)
RELAYED = (1, 7, 2, 6)
DIRECT = (4, 3, 5)


def position():
    blk = lax.axis_index("blk")
    slab = lax.axis_index("slab")
    z = blk // 4
    y = ((blk // 2) % 2) * 2 + slab % 2
    return slab // 2, y, z, blk % 2


def device(x, y, z, core):
    return {"blk": (z * 2 + y // 2) * 2 + core, "slab": x * 2 + y % 2}


def iota(shape, dim):
    return lax.broadcasted_iota(I32, shape, dim)


def split3(value):
    first = value.astype(BF16)
    rest = value - first.astype(F32)
    second = rest.astype(BF16)
    third = (rest - second.astype(F32)).astype(BF16)
    return first, second, third


def kernel(
    stride,
    scale,
    q_hbm,
    w_hbm,
    id_hbm,
    pas_ref,
    loss_ref,
    grad_ref,
    q_ref,
    w_ref,
    id_ref,
    pas,
    pas_t,
    queries,
    cands,
    cand_out,
    perm_ref,
    prob_out,
    exp_out,
    stat_out,
    prob_in,
    line_out,
    line_in,
    exp_in,
    stat_in,
    z_out,
    z_in,
    zstat_out,
    zstat_in,
    in_sems,
    pas_sem,
    q_sems,
    c_sems,
    prob_sems,
    exp_sems,
    stat_sems,
    z_sems,
    zstat_sems,
):
    x, y, z, core = position()
    y_hi, y_lo = y // 2, y % 2
    slab = x * 2 + y_lo
    width = pas_ref.shape[0]
    num_cand = id_ref.shape[1]
    plane = width * 32
    per_plane = plane // stride

    plane_to = [
        (
            device((x + ex) % 4, ((y_hi + dy) % 2) * 2 + (y_lo + eyl) % 2, z, core),
            dy * 8 + ex * 2 + eyl,
            dy * 8 + ((4 - ex) % 4) * 2 + eyl,
        )
        for dy in (0, 1)
        for ex in (2, 1, 3, 0)
        for eyl in (0, 1)
        if (dy, ex, eyl) != (0, 0, 0)
    ]
    z_to = [(device(x, y, (z + d) % 8, core), d, (8 - d) % 8) for d in FAR_FIRST]
    other = device(x, y, z, 1 - core)

    barrier = pltpu.get_barrier_semaphore()
    greeted = [p[0] for p in plane_to] + [other]
    greeted = [device(x, 3 - y, (z + d) % 8, core) for d in FAR_FIRST] + greeted
    greeted = [p[0] for p in z_to] + greeted
    for target in greeted:
        pl.semaphore_signal(barrier, inc=1, device_id=target, device_id_type=MESH)

    small = [
        pltpu.make_async_copy(src, dst, in_sems.at[i])
        for i, (src, dst) in enumerate(((w_hbm, w_ref), (id_hbm, id_ref), (q_hbm, q_ref)))
    ]
    for copy in small:
        copy.start()
    load = pltpu.make_async_copy(pas_ref, pas.at[0], pas_sem.at[0])
    load.start()
    for copy in small:
        copy.wait()

    weights = w_ref[...].astype(F32)
    weight_sum = jnp.sum(weights, axis=1, keepdims=True)
    own_prob = weights / weight_sum
    entropy = jnp.sum(own_prob * jnp.log(own_prob), axis=1, keepdims=True)
    pad = 256 - num_cand
    wide_w = jnp.concatenate([weights, jnp.zeros((16, pad), F32)], axis=1)
    wide_id = jnp.concatenate([id_ref[...], jnp.zeros((16, pad), I32)], axis=1)
    s1, s2, s3 = split3(weight_sum)
    lane32 = iota((16, 32), 1)
    sums = jnp.where(
        lane32 == 0,
        s1.astype(F32),
        jnp.where(lane32 == 1, s2.astype(F32), jnp.where(lane32 == 2, s3.astype(F32), 0.0)),
    )
    for zz in range(8):
        lo = per_plane * zz
        ids = jnp.maximum(wide_id[:, lo : lo + 32] - lo * stride, 0)
        high = (ids >> 8).astype(F32)
        low = (ids & 255).astype(F32)
        cand_out[zz] = jnp.concatenate([high, low, wide_w[:, lo : lo + 32], sums], axis=1).astype(BF16)
    cands[0] = cand_out[z]
    queries[0] = q_ref[...]

    pl.semaphore_wait(barrier, len(greeted))

    swap = pltpu.make_async_remote_copy(
        pas_ref, pas.at[1], pas_sem.at[1], pas_sem.at[2], device_id=other, device_id_type=MESH
    )
    swap.start()
    sent = []
    mirror = device(x, 3 - y, z, core)

    def send(src, dst, sems, i, target):
        copy = pltpu.make_async_remote_copy(
            src, dst, sems.at[0, i], sems.at[1, i], device_id=target, device_id_type=MESH
        )
        copy.start()
        sent.append(copy)
        return copy

    cand_copies, near_copies, low_copies, high_copies = [], {}, [], []
    for d in FAR_FIRST + (0,):
        for dy in (0, 1):
            if d or dy:
                target = device(x, 3 - y if dy else y, (z + d) % 8, core)
                slot = dy * 8 + (8 - d) % 8
                cand_copies.append(send(cand_out.at[(z + d) % 8], cands.at[slot], c_sems, slot, target))
    for d in RELAYED:
        target = device(x, y, (z + d) % 8, core)
        near_copies[d] = send(q_ref, queries.at[8 - d], q_sems, d, target)
    for d in DIRECT:
        target = device(x, y, (z + d) % 8, core)
        low_copies.append(send(q_ref, queries.at[8 - d], q_sems, d, target))
    for d in DIRECT:
        target = device(x, 3 - y, (z + d) % 8, core)
        high_copies.append(send(q_ref, queries.at[16 - d], q_sems, 8 + d, target))
    high_copies.append(send(q_ref, queries.at[8], q_sems, 8, mirror))
    p_row = iota((128, 1), 0)
    p_x = (x + (p_row >> 5)) & 3
    p_y = (y_lo + ((p_row >> 4) & 1)) & 1
    p_n = ((p_row >> 1) & 7) * 16 + (p_x * 2 + p_y) * 2 + (p_row & 1)
    mask = iota((128, 128), 1) == p_n
    perm_ref[...] = mask.astype(F32).astype(BF16)

    offsets = [((((z * 2 + y_hi) * 2 + c) * 8) + slab) * width for c in (core, 1 - core)]
    firsts = [jnp.minimum(off // stride, num_cand - 2) - per_plane * z for off in offsets]
    out_lane = iota((1, 128), 1)
    target_lane = jnp.where((out_lane >= 12) & (out_lane < 15), 96 + out_lane - 12, -1)
    for rho in range(2):
        for c in range(2):
            for field in range(3):
                target_lane = jnp.where(
                    out_lane == (rho * 2 + c) * 3 + field, field * 32 + firsts[rho] + c, target_lane
                )
    pick = (iota((128, 128), 0) == target_lane).astype(F32).astype(BF16)
    load.wait()
    pas_t[0] = pas[0].T
    for d in RELAYED:
        near_copies[d].wait_recv()
        high_copies.append(send(queries.at[8 - d], queries.at[16 - d], q_sems, 8 + d, mirror))

    swap.wait_recv()
    pas_t[1] = pas[1].T

    for copy in cand_copies:
        copy.wait_recv()
    picked = jnp.dot(cands[...].reshape(256, 128), pick, preferred_element_type=F32).astype(BF16)
    picked = jnp.concatenate(
        [
            jnp.dot(perm_ref[...], picked[h * 128 : h * 128 + 128], preferred_element_type=F32)
            for h in range(2)
        ],
        axis=0,
    )
    total_w = picked[:, 12:13] + picked[:, 13:14] + picked[:, 14:15]
    column = iota((256, width), 1).astype(F32)
    prob_sum = None
    for rho in range(2):
        shift = (per_plane * stride * z - offsets[rho]).astype(F32)
        dense = None
        for c in range(2):
            at = (rho * 2 + c) * 3
            local = picked[:, at : at + 1] * 256.0 + picked[:, at + 1 : at + 2] + shift
            prob = picked[:, at + 2 : at + 3] / total_w
            term = jnp.where(column == local, prob, 0.0)
            dense = term if dense is None else dense + term
        part = jnp.dot(dense.astype(BF16), pas[rho], preferred_element_type=F32)
        prob_sum = part if prob_sum is None else prob_sum + part
    groups = prob_sum.astype(BF16).reshape(2, 4, 2, 16, -1)
    for dy in range(2):
        for ex in range(4):
            prob_out[ex, dy * 2 : dy * 2 + 2] = groups[dy, ex]
    prob_copies = [
        send(prob_out.at[ex], prob_in.at[4 - ex], prob_sems, ex, device((x + ex) % 4, y, z, core))
        for ex in (2, 1, 3)
    ]

    depth = q_ref.shape[1]
    exp_copies, stat_copies = [], []
    for h, waits in enumerate((low_copies, high_copies)):
        for copy in waits:
            copy.wait_recv()
        half = queries[h * 8 : h * 8 + 8].reshape(128, depth)
        rows = jnp.dot(perm_ref[...], half, preferred_element_type=F32)
        rows16 = rows.astype(BF16)
        scores = [
            scale * jnp.dot(rows16, pas_t[rho], preferred_element_type=F32)
            for rho in range(2)
        ]
        peak = jnp.maximum(
            jnp.max(scores[0], axis=1, keepdims=True), jnp.max(scores[1], axis=1, keepdims=True)
        )
        exps = [jnp.exp(s - peak) for s in scores]
        mixed = jnp.dot(exps[0].astype(BF16), pas[0], preferred_element_type=F32) + jnp.dot(
            exps[1].astype(BF16), pas[1], preferred_element_type=F32
        )
        exp_out[h * 8 : h * 8 + 8] = mixed.astype(BF16).reshape(8, 16, depth)
        for i, (target, group, slot) in enumerate(plane_to):
            if group // 8 == h:
                exp_copies.append(send(exp_out.at[group], exp_in.at[slot], exp_sems, i, target))
        total = jnp.sum(exps[0], axis=1, keepdims=True) + jnp.sum(exps[1], axis=1, keepdims=True)
        teacher = scale * jnp.sum(rows * prob_sum[h * 128 : h * 128 + 128], axis=1, keepdims=True)
        for k, stat in enumerate((peak, total, teacher)):
            stat_out[h, k : k + 1, :] = jnp.sum(jnp.where(mask, stat, 0.0), axis=0, keepdims=True)
        for i, (target, group, slot) in enumerate(plane_to):
            if group // 8 == h:
                stat_copies.append(send(stat_out.at[h], stat_in.at[slot], stat_sems, i, target))

    stat_in[0] = stat_out[0]
    o = iota((384, 1), 0)
    d_of = o // 48
    j = o - 48 * d_of
    part = j // 12
    jj = j - 12 * part
    source = part * 96 + (jj >> 1) * 16 + d_of * 2 + (jj & 1)
    order = (iota((384, 384), 1) == source).astype(F32).astype(BF16)
    entropy_lanes = jnp.sum(
        jnp.where(iota((16, 16), 0) == iota((16, 16), 1), entropy, 0.0), axis=0, keepdims=True
    )
    for copy in prob_copies:
        copy.wait_recv()
    prob_rows = prob_out[0].astype(F32)
    for i in range(1, 4):
        prob_rows = prob_rows + prob_in[i].astype(F32)
    line_out[...] = prob_rows.astype(BF16)
    prob_rows = prob_rows[0]
    line_copies = []
    for k in (2, 3, 1):
        target = device(x, ((y_hi + k // 2) % 2) * 2 + (y_lo + k % 2) % 2, z, core)
        line_copies.append(send(line_out.at[k], line_in.at[k], prob_sems, 3 + k, target))
    for copy in stat_copies:
        copy.wait_recv()
    peaks = jnp.concatenate([stat_in[i, 0:1, :] for i in range(16)], axis=0)
    totals = jnp.concatenate([stat_in[i, 1:2, :] for i in range(16)], axis=0)
    teachers = jnp.concatenate([stat_in[i, 2:3, :] for i in range(16)], axis=0)
    peak = jnp.max(peaks, axis=0, keepdims=True)
    share = jnp.exp(peaks - peak)
    total = jnp.sum(totals * share, axis=0, keepdims=True)
    teacher = jnp.sum(teachers, axis=0, keepdims=True)
    zstat_out[0:1, :] = peak
    zstat_out[1:2, :] = total
    zstat_out[2:3, :] = teacher
    zstat_copies = [
        send(zstat_out, zstat_in.at[slot], zstat_sems, i, target)
        for i, (target, d, slot) in enumerate(z_to)
    ]
    row = iota((16, 128), 0)
    own_lane = iota((16, 128), 1) == (row >> 1) * 16 + slab * 2 + (row & 1)
    columns = [
        jnp.sum(jnp.where(own_lane, share[i : i + 1, :], 0.0), axis=1, keepdims=True) for i in range(16)
    ]
    exp_rows = exp_out[0].astype(F32) * columns[0]
    for copy, (_, _, slot) in zip(exp_copies, plane_to):
        copy.wait_recv()
        exp_rows = exp_rows + exp_in[slot].astype(F32) * columns[slot]

    for copy in line_copies:
        copy.wait_recv()
    for k in range(1, 4):
        prob_rows = prob_rows + line_in[k].astype(F32)

    stacked = jnp.concatenate(
        [part[:, b * 128 : (b + 1) * 128] for part in (exp_rows, prob_rows) for b in range(6)], axis=0
    )
    coarse = stacked.astype(BF16)
    fine = (stacked - coarse.astype(F32)).astype(BF16)
    stacked = jnp.concatenate([coarse, fine], axis=0)
    z_out[...] = jnp.dot(order, stacked, preferred_element_type=F32).astype(BF16).reshape(8, 48, 128)
    z_copies = [
        send(z_out.at[d], z_in.at[slot], z_sems, i, target) for i, (target, d, slot) in enumerate(z_to)
    ]

    zstat_in[0] = zstat_out[...]
    for copy in zstat_copies:
        copy.wait_recv()

    def gathered(k):
        return jnp.concatenate(
            [zstat_in[s, k : k + 1, ((8 - s) % 8) * 16 : ((8 - s) % 8) * 16 + 16] for s in range(8)], axis=0
        )

    peaks, totals, teachers = gathered(0), gathered(1), gathered(2)
    peak = jnp.max(peaks, axis=0, keepdims=True)
    total = jnp.sum(totals * jnp.exp(peaks - peak), axis=0, keepdims=True)
    lse = peak + jnp.log(total)
    loss_ref[...] = entropy_lanes - jnp.sum(teachers, axis=0, keepdims=True) + lse
    share = jnp.exp(peaks - lse)
    row = iota((16, 16), 0)
    own_lane = iota((16, 16), 1) == slab * 2 + (row & 1)
    columns = [
        jnp.sum(jnp.where(own_lane, share[s : s + 1, :], 0.0), axis=1, keepdims=True) for s in range(8)
    ]
    for copy in z_copies:
        copy.wait_recv()
    z_in[0] = z_out[0]
    result = None
    for s in range(8):
        block = z_in[s].astype(F32)
        block = block[0:24] + block[24:48]
        term = block[0:12] * columns[s][0:12] - block[12:24]
        result = term if result is None else result + term
    result = scale * result
    for b in range(6):
        grad_ref[:, b * 128 : (b + 1) * 128] = result[2 * b : 2 * b + 2]

    swap.wait_send()
    for copy in sent:
        copy.wait_send()


def shards(queries, teacher_weight, cand_ids, passages):
    rows, depth = queries.shape
    width = passages.shape[0]
    num_cand = cand_ids.shape[1]
    stride = width * 256 // num_cand
    scale = 3.0 / math.sqrt(depth)
    vmem = pl.BlockSpec(memory_space=pltpu.VMEM)
    dma = pltpu.SemaphoreType.DMA
    loss, grad = pl.pallas_call(
        functools.partial(kernel, stride, scale),
        out_shape=(pltpu.VMEM((1, rows), F32), pltpu.VMEM((2, depth), F32)),
        in_specs=[pl.BlockSpec(memory_space=pltpu.HBM)] * 4,
        out_specs=(vmem, vmem),
        scratch_shapes=[
            pltpu.VMEM((rows, depth), BF16),
            pltpu.VMEM((rows, num_cand), BF16),
            pltpu.VMEM((rows, num_cand), I32),
            pltpu.VMEM((2, width, depth), BF16),
            pltpu.VMEM((2, depth, width), BF16),
            pltpu.VMEM((16, 16, depth), BF16),
            pltpu.VMEM((16, 16, 128), BF16),
            pltpu.VMEM((8, 16, 128), BF16),
            pltpu.VMEM((128, 128), BF16),
            pltpu.VMEM((4, 4, 16, depth), BF16),
            pltpu.VMEM((16, 16, depth), BF16),
            pltpu.VMEM((2, 8, 128), F32),
            pltpu.VMEM((4, 4, 16, depth), BF16),
            pltpu.VMEM((4, 16, depth), BF16),
            pltpu.VMEM((4, 16, depth), BF16),
            pltpu.VMEM((16, 16, depth), BF16),
            pltpu.VMEM((16, 8, 128), F32),
            pltpu.VMEM((8, 48, 128), BF16),
            pltpu.VMEM((8, 48, 128), BF16),
            pltpu.VMEM((8, 128), F32),
            pltpu.VMEM((8, 8, 128), F32),
            dma((3,)),
            dma((3,)),
            dma((2, 16)),
            dma((2, 16)),
            dma((2, 15)),
            dma((2, 15)),
            dma((2, 15)),
            dma((2, 7)),
            dma((2, 7)),
        ],
        compiler_params=pltpu.CompilerParams(
            collective_id=0, has_side_effects=True, vmem_limit_bytes=60 * 1024 * 1024
        ),
    )(*(pltpu.with_memory_space_constraint(a, pltpu.HBM) for a in (queries, teacher_weight, cand_ids, passages)))
    return (loss.reshape(rows), grad)


def solution(mesh):
    return jax.shard_map(
        shards,
        mesh=mesh,
        in_specs=(P("blk", None), P("blk", None), P("blk", None), P(("blk", "slab"), None)),
        out_specs=(P("blk"), P(("blk", "slab"), None)),
        check_vma=False,
    )
```

```python
import functools
import math

import jax
import jax.numpy as jnp
from jax import lax
from jax.experimental import pallas as pl
from jax.experimental.pallas import tpu as pltpu
from jax.sharding import PartitionSpec as P

MESH = pl.DeviceIdType.MESH
F32 = jnp.float32
BF16 = jnp.bfloat16
I32 = jnp.int32
FAR_FIRST = (4, 3, 5, 2, 6, 1, 7)
RELAYED = (1, 7, 2, 6)
DIRECT = (4, 3, 5)


def position():
    blk = lax.axis_index("blk")
    slab = lax.axis_index("slab")
    z = blk // 4
    y = ((blk // 2) % 2) * 2 + slab % 2
    return slab // 2, y, z, blk % 2


def device(x, y, z, core):
    return {"blk": (z * 2 + y // 2) * 2 + core, "slab": x * 2 + y % 2}


def iota(shape, dim):
    return lax.broadcasted_iota(I32, shape, dim)


def split3(value):
    first = value.astype(BF16)
    rest = value - first.astype(F32)
    second = rest.astype(BF16)
    third = (rest - second.astype(F32)).astype(BF16)
    return first, second, third


def kernel(
    stride,
    scale,
    q_hbm,
    w_hbm,
    id_hbm,
    pas_ref,
    loss_ref,
    grad_ref,
    q_ref,
    w_ref,
    id_ref,
    pas,
    pas_t,
    queries,
    cands,
    cand_out,
    perm_ref,
    prob_out,
    exp_out,
    stat_out,
    prob_in,
    line_out,
    line_in,
    exp_in,
    stat_in,
    z_out,
    z_in,
    zstat_out,
    zstat_in,
    in_sems,
    pas_sem,
    q_sems,
    c_sems,
    prob_sems,
    exp_sems,
    stat_sems,
    z_sems,
    zstat_sems,
):
    x, y, z, core = position()
    y_hi, y_lo = y // 2, y % 2
    slab = x * 2 + y_lo
    width = pas_ref.shape[0]
    num_cand = id_ref.shape[1]
    plane = width * 32
    per_plane = plane // stride

    plane_to = [
        (
            device((x + ex) % 4, ((y_hi + dy) % 2) * 2 + (y_lo + eyl) % 2, z, core),
            dy * 8 + ex * 2 + eyl,
            dy * 8 + ((4 - ex) % 4) * 2 + eyl,
        )
        for dy in (0, 1)
        for ex in (2, 1, 3, 0)
        for eyl in (0, 1)
        if (dy, ex, eyl) != (0, 0, 0)
    ]
    z_to = [(device(x, y, (z + d) % 8, core), d, (8 - d) % 8) for d in FAR_FIRST]
    other = device(x, y, z, 1 - core)

    barrier = pltpu.get_barrier_semaphore()
    greeted = [p[0] for p in plane_to] + [other]
    greeted = [device(x, 3 - y, (z + d) % 8, core) for d in FAR_FIRST] + greeted
    greeted = [p[0] for p in z_to] + greeted
    for target in greeted:
        pl.semaphore_signal(barrier, inc=1, device_id=target, device_id_type=MESH)

    small = [
        pltpu.make_async_copy(src, dst, in_sems.at[i])
        for i, (src, dst) in enumerate(((w_hbm, w_ref), (id_hbm, id_ref), (q_hbm, q_ref)))
    ]
    for copy in small:
        copy.start()
    load = pltpu.make_async_copy(pas_ref, pas.at[0], pas_sem.at[0])
    load.start()
    for copy in small:
        copy.wait()

    weights = w_ref[...].astype(F32)
    weight_sum = jnp.sum(weights, axis=1, keepdims=True)
    own_prob = weights / weight_sum
    entropy = jnp.sum(own_prob * jnp.log(own_prob), axis=1, keepdims=True)
    pad = 256 - num_cand
    wide_w = jnp.concatenate([weights, jnp.zeros((16, pad), F32)], axis=1)
    wide_id = jnp.concatenate([id_ref[...], jnp.zeros((16, pad), I32)], axis=1)
    s1, s2, s3 = split3(weight_sum)
    lane32 = iota((16, 32), 1)
    sums = jnp.where(
        lane32 == 0,
        s1.astype(F32),
        jnp.where(lane32 == 1, s2.astype(F32), jnp.where(lane32 == 2, s3.astype(F32), 0.0)),
    )
    for zz in range(8):
        lo = per_plane * zz
        ids = jnp.maximum(wide_id[:, lo : lo + 32] - lo * stride, 0)
        high = (ids >> 8).astype(F32)
        low = (ids & 255).astype(F32)
        cand_out[zz] = jnp.concatenate([high, low, wide_w[:, lo : lo + 32], sums], axis=1).astype(BF16)
    cands[0] = cand_out[z]
    queries[0] = q_ref[...]

    pl.semaphore_wait(barrier, len(greeted))

    swap = pltpu.make_async_remote_copy(
        pas_ref, pas.at[1], pas_sem.at[1], pas_sem.at[2], device_id=other, device_id_type=MESH
    )
    swap.start()
    sent = []
    mirror = device(x, 3 - y, z, core)

    def send(src, dst, sems, i, target):
        copy = pltpu.make_async_remote_copy(
            src, dst, sems.at[0, i], sems.at[1, i], device_id=target, device_id_type=MESH
        )
        copy.start()
        sent.append(copy)
        return copy

    cand_copies, near_copies, low_copies, high_copies = [], {}, [], []
    for d in FAR_FIRST + (0,):
        for dy in (0, 1):
            if d or dy:
                target = device(x, 3 - y if dy else y, (z + d) % 8, core)
                slot = dy * 8 + (8 - d) % 8
                cand_copies.append(send(cand_out.at[(z + d) % 8], cands.at[slot], c_sems, slot, target))
    for d in RELAYED:
        target = device(x, y, (z + d) % 8, core)
        near_copies[d] = send(q_ref, queries.at[8 - d], q_sems, d, target)
    for d in DIRECT:
        target = device(x, y, (z + d) % 8, core)
        low_copies.append(send(q_ref, queries.at[8 - d], q_sems, d, target))
    for d in DIRECT:
        target = device(x, 3 - y, (z + d) % 8, core)
        high_copies.append(send(q_ref, queries.at[16 - d], q_sems, 8 + d, target))
    high_copies.append(send(q_ref, queries.at[8], q_sems, 8, mirror))
    p_row = iota((128, 1), 0)
    p_x = (x + (p_row >> 5)) & 3
    p_y = (y_lo + ((p_row >> 4) & 1)) & 1
    p_n = ((p_row >> 1) & 7) * 16 + (p_x * 2 + p_y) * 2 + (p_row & 1)
    mask = iota((128, 128), 1) == p_n
    perm_ref[...] = mask.astype(F32).astype(BF16)

    offsets = [((((z * 2 + y_hi) * 2 + c) * 8) + slab) * width for c in (core, 1 - core)]
    firsts = [jnp.minimum(off // stride, num_cand - 2) - per_plane * z for off in offsets]
    out_lane = iota((1, 128), 1)
    target_lane = jnp.where((out_lane >= 12) & (out_lane < 15), 96 + out_lane - 12, -1)
    for rho in range(2):
        for c in range(2):
            for field in range(3):
                target_lane = jnp.where(
                    out_lane == (rho * 2 + c) * 3 + field, field * 32 + firsts[rho] + c, target_lane
                )
    pick = (iota((128, 128), 0) == target_lane).astype(F32).astype(BF16)
    load.wait()
    pas_t[0] = pas[0].T
    for copy in cand_copies:
        copy.wait_recv()
    picked = jnp.dot(cands[...].reshape(256, 128), pick, preferred_element_type=F32).astype(BF16)
    picked = jnp.concatenate(
        [
            jnp.dot(perm_ref[...], picked[h * 128 : h * 128 + 128], preferred_element_type=F32)
            for h in range(2)
        ],
        axis=0,
    )
    total_w = picked[:, 12:13] + picked[:, 13:14] + picked[:, 14:15]
    for d in RELAYED:
        near_copies[d].wait_recv()
        high_copies.append(send(queries.at[8 - d], queries.at[16 - d], q_sems, 8 + d, mirror))

    swap.wait_recv()
    pas_t[1] = pas[1].T

    column = iota((128, width), 1).astype(F32)
    prob_copies, prob_sums = [], []
    for h in range(2):
        mine = slice(h * 128, h * 128 + 128)
        prob_sum = None
        for rho in range(2):
            shift = (per_plane * stride * z - offsets[rho]).astype(F32)
            dense = 0.0
            for c in range(2):
                at = (rho * 2 + c) * 3
                local = picked[mine, at : at + 1] * 256.0 + picked[mine, at + 1 : at + 2] + shift
                prob = picked[mine, at + 2 : at + 3] / total_w[mine]
                dense = jnp.where(column == local, prob, dense)
            part = jnp.dot(dense.astype(BF16), pas[rho], preferred_element_type=F32)
            prob_sum = part if prob_sum is None else prob_sum + part
        prob_sums.append(prob_sum)
        groups = prob_sum.astype(BF16).reshape(4, 2, 16, -1)
        span = pl.ds(h * 2, 2)
        for ex in (2, 1, 3, 0):
            prob_out[ex, span] = groups[ex]
            if ex:
                target = device((x + ex) % 4, y, z, core)
                prob_copies.append(
                    send(prob_out.at[ex, span], prob_in.at[4 - ex, span], prob_sems, ex + 4 * h, target)
                )

    depth = q_ref.shape[1]
    exp_copies, stat_copies = [], []
    for h, waits in enumerate((low_copies, high_copies)):
        for copy in waits:
            copy.wait_recv()
        half = queries[h * 8 : h * 8 + 8].reshape(128, depth)
        rows = jnp.dot(perm_ref[...], half, preferred_element_type=F32)
        rows16 = rows.astype(BF16)
        scores = [
            scale * jnp.dot(rows16, pas_t[rho], preferred_element_type=F32)
            for rho in range(2)
        ]
        peak = jnp.maximum(
            jnp.max(scores[0], axis=1, keepdims=True), jnp.max(scores[1], axis=1, keepdims=True)
        )
        exps = [jnp.exp(s - peak) for s in scores]
        mixed = jnp.dot(exps[0].astype(BF16), pas[0], preferred_element_type=F32) + jnp.dot(
            exps[1].astype(BF16), pas[1], preferred_element_type=F32
        )
        exp_out[h * 8 : h * 8 + 8] = mixed.astype(BF16).reshape(8, 16, depth)
        for i, (target, group, slot) in enumerate(plane_to):
            if group // 8 == h:
                exp_copies.append(send(exp_out.at[group], exp_in.at[slot], exp_sems, i, target))
        total = jnp.sum(exps[0], axis=1, keepdims=True) + jnp.sum(exps[1], axis=1, keepdims=True)
        teacher = scale * jnp.sum(rows * prob_sums[h], axis=1, keepdims=True)
        for k, stat in enumerate((peak, total, teacher)):
            stat_out[h, k : k + 1, :] = jnp.sum(jnp.where(mask, stat, 0.0), axis=0, keepdims=True)
        for i, (target, group, slot) in enumerate(plane_to):
            if group // 8 == h:
                stat_copies.append(send(stat_out.at[h], stat_in.at[slot], stat_sems, i, target))

    stat_in[0] = stat_out[0]
    o = iota((384, 1), 0)
    d_of = o // 48
    j = o - 48 * d_of
    part = j // 12
    jj = j - 12 * part
    source = part * 96 + (jj >> 1) * 16 + d_of * 2 + (jj & 1)
    order = (iota((384, 384), 1) == source).astype(F32).astype(BF16)
    entropy_lanes = jnp.sum(
        jnp.where(iota((16, 16), 0) == iota((16, 16), 1), entropy, 0.0), axis=0, keepdims=True
    )
    for copy in prob_copies:
        copy.wait_recv()
    prob_rows = prob_out[0].astype(F32)
    for i in range(1, 4):
        prob_rows = prob_rows + prob_in[i].astype(F32)
    line_out[...] = prob_rows.astype(BF16)
    prob_rows = prob_rows[0]
    line_copies = []
    for k in (2, 3, 1):
        target = device(x, ((y_hi + k // 2) % 2) * 2 + (y_lo + k % 2) % 2, z, core)
        line_copies.append(send(line_out.at[k], line_in.at[k], prob_sems, 7 + k, target))
    for copy in stat_copies:
        copy.wait_recv()
    peaks = jnp.concatenate([stat_in[i, 0:1, :] for i in range(16)], axis=0)
    totals = jnp.concatenate([stat_in[i, 1:2, :] for i in range(16)], axis=0)
    teachers = jnp.concatenate([stat_in[i, 2:3, :] for i in range(16)], axis=0)
    peak = jnp.max(peaks, axis=0, keepdims=True)
    share = jnp.exp(peaks - peak)
    total = jnp.sum(totals * share, axis=0, keepdims=True)
    teacher = jnp.sum(teachers, axis=0, keepdims=True)
    zstat_out[0:1, :] = peak
    zstat_out[1:2, :] = total
    zstat_out[2:3, :] = teacher
    zstat_copies = [
        send(zstat_out, zstat_in.at[slot], zstat_sems, i, target)
        for i, (target, d, slot) in enumerate(z_to)
    ]
    row = iota((16, 128), 0)
    own_lane = iota((16, 128), 1) == (row >> 1) * 16 + slab * 2 + (row & 1)
    columns = [
        jnp.sum(jnp.where(own_lane, share[i : i + 1, :], 0.0), axis=1, keepdims=True) for i in range(16)
    ]
    exp_rows = exp_out[0].astype(F32) * columns[0]
    for copy, (_, _, slot) in zip(exp_copies, plane_to):
        copy.wait_recv()
        exp_rows = exp_rows + exp_in[slot].astype(F32) * columns[slot]

    for copy in line_copies:
        copy.wait_recv()
    for k in range(1, 4):
        prob_rows = prob_rows + line_in[k].astype(F32)

    stacked = jnp.concatenate(
        [part[:, b * 128 : (b + 1) * 128] for part in (exp_rows, prob_rows) for b in range(6)], axis=0
    )
    coarse = stacked.astype(BF16)
    fine = (stacked - coarse.astype(F32)).astype(BF16)
    stacked = jnp.concatenate([coarse, fine], axis=0)
    z_out[...] = jnp.dot(order, stacked, preferred_element_type=F32).astype(BF16).reshape(8, 48, 128)
    z_copies = [
        send(z_out.at[d], z_in.at[slot], z_sems, i, target) for i, (target, d, slot) in enumerate(z_to)
    ]

    zstat_in[0] = zstat_out[...]
    for copy in zstat_copies:
        copy.wait_recv()

    def gathered(k):
        return jnp.concatenate(
            [zstat_in[s, k : k + 1, ((8 - s) % 8) * 16 : ((8 - s) % 8) * 16 + 16] for s in range(8)], axis=0
        )

    peaks, totals, teachers = gathered(0), gathered(1), gathered(2)
    peak = jnp.max(peaks, axis=0, keepdims=True)
    total = jnp.sum(totals * jnp.exp(peaks - peak), axis=0, keepdims=True)
    lse = peak + jnp.log(total)
    loss_ref[...] = entropy_lanes - jnp.sum(teachers, axis=0, keepdims=True) + lse
    share = jnp.exp(peaks - lse)
    row = iota((16, 16), 0)
    own_lane = iota((16, 16), 1) == slab * 2 + (row & 1)
    columns = [
        jnp.sum(jnp.where(own_lane, share[s : s + 1, :], 0.0), axis=1, keepdims=True) for s in range(8)
    ]
    for copy in z_copies:
        copy.wait_recv()
    z_in[0] = z_out[0]
    result = None
    for s in range(8):
        block = z_in[s].astype(F32)
        block = block[0:24] + block[24:48]
        term = block[0:12] * columns[s][0:12] - block[12:24]
        result = term if result is None else result + term
    result = scale * result
    for b in range(6):
        grad_ref[:, b * 128 : (b + 1) * 128] = result[2 * b : 2 * b + 2]

    swap.wait_send()
    for copy in sent:
        copy.wait_send()


def shards(queries, teacher_weight, cand_ids, passages):
    rows, depth = queries.shape
    width = passages.shape[0]
    num_cand = cand_ids.shape[1]
    stride = width * 256 // num_cand
    scale = 3.0 / math.sqrt(depth)
    vmem = pl.BlockSpec(memory_space=pltpu.VMEM)
    dma = pltpu.SemaphoreType.DMA
    loss, grad = pl.pallas_call(
        functools.partial(kernel, stride, scale),
        out_shape=(pltpu.VMEM((1, rows), F32), pltpu.VMEM((2, depth), F32)),
        in_specs=[pl.BlockSpec(memory_space=pltpu.HBM)] * 4,
        out_specs=(vmem, vmem),
        scratch_shapes=[
            pltpu.VMEM((rows, depth), BF16),
            pltpu.VMEM((rows, num_cand), BF16),
            pltpu.VMEM((rows, num_cand), I32),
            pltpu.VMEM((2, width, depth), BF16),
            pltpu.VMEM((2, depth, width), BF16),
            pltpu.VMEM((16, 16, depth), BF16),
            pltpu.VMEM((16, 16, 128), BF16),
            pltpu.VMEM((8, 16, 128), BF16),
            pltpu.VMEM((128, 128), BF16),
            pltpu.VMEM((4, 4, 16, depth), BF16),
            pltpu.VMEM((16, 16, depth), BF16),
            pltpu.VMEM((2, 8, 128), F32),
            pltpu.VMEM((4, 4, 16, depth), BF16),
            pltpu.VMEM((4, 16, depth), BF16),
            pltpu.VMEM((4, 16, depth), BF16),
            pltpu.VMEM((16, 16, depth), BF16),
            pltpu.VMEM((16, 8, 128), F32),
            pltpu.VMEM((8, 48, 128), BF16),
            pltpu.VMEM((8, 48, 128), BF16),
            pltpu.VMEM((8, 128), F32),
            pltpu.VMEM((8, 8, 128), F32),
            dma((3,)),
            dma((3,)),
            dma((2, 16)),
            dma((2, 16)),
            dma((2, 15)),
            dma((2, 15)),
            dma((2, 15)),
            dma((2, 7)),
            dma((2, 7)),
        ],
        compiler_params=pltpu.CompilerParams(
            collective_id=0, has_side_effects=True, vmem_limit_bytes=60 * 1024 * 1024
        ),
    )(*(pltpu.with_memory_space_constraint(a, pltpu.HBM) for a in (queries, teacher_weight, cand_ids, passages)))
    return (loss.reshape(rows), grad)


def solution(mesh):
    return jax.shard_map(
        shards,
        mesh=mesh,
        in_specs=(P("blk", None), P("blk", None), P("blk", None), P(("blk", "slab"), None)),
        out_specs=(P("blk"), P(("blk", "slab"), None)),
        check_vma=False,
    )
```

```python
import functools
import math

import jax
import jax.numpy as jnp
from jax import lax
from jax.experimental import pallas as pl
from jax.experimental.pallas import tpu as pltpu
from jax.sharding import PartitionSpec as P

MESH = pl.DeviceIdType.MESH
F32 = jnp.float32
BF16 = jnp.bfloat16
I32 = jnp.int32
FAR_FIRST = (4, 3, 5, 2, 6, 1, 7)
RELAYED = (2, 6)
DIRECT = (4, 3, 5, 1, 7)


def position():
    blk = lax.axis_index("blk")
    slab = lax.axis_index("slab")
    z = blk // 4
    y = ((blk // 2) % 2) * 2 + slab % 2
    return slab // 2, y, z, blk % 2


def device(x, y, z, core):
    return {"blk": (z * 2 + y // 2) * 2 + core, "slab": x * 2 + y % 2}


def iota(shape, dim):
    return lax.broadcasted_iota(I32, shape, dim)


def split3(value):
    first = value.astype(BF16)
    rest = value - first.astype(F32)
    second = rest.astype(BF16)
    third = (rest - second.astype(F32)).astype(BF16)
    return first, second, third


def kernel(
    stride,
    scale,
    q_hbm,
    w_hbm,
    id_hbm,
    pas_ref,
    loss_ref,
    grad_ref,
    q_ref,
    w_ref,
    id_ref,
    pas,
    pas_t,
    queries,
    cands,
    cand_out,
    perm_ref,
    prob_out,
    exp_out,
    stat_out,
    prob_in,
    line_out,
    line_in,
    exp_in,
    stat_in,
    z_out,
    z_in,
    zstat_out,
    zstat_in,
    in_sems,
    pas_sem,
    q_sems,
    c_sems,
    prob_sems,
    exp_sems,
    stat_sems,
    z_sems,
    zstat_sems,
):
    x, y, z, core = position()
    y_hi, y_lo = y // 2, y % 2
    slab = x * 2 + y_lo
    width = pas_ref.shape[0]
    num_cand = id_ref.shape[1]
    plane = width * 32
    per_plane = plane // stride

    plane_to = [
        (
            device((x + ex) % 4, ((y_hi + dy) % 2) * 2 + (y_lo + eyl) % 2, z, core),
            dy * 8 + ex * 2 + eyl,
            dy * 8 + ((4 - ex) % 4) * 2 + eyl,
        )
        for dy in (0, 1)
        for ex in (2, 1, 3, 0)
        for eyl in (0, 1)
        if (dy, ex, eyl) != (0, 0, 0)
    ]
    z_to = [(device(x, y, (z + d) % 8, core), d, (8 - d) % 8) for d in FAR_FIRST]
    other = device(x, y, z, 1 - core)

    barrier = pltpu.get_barrier_semaphore()
    greeted = [p[0] for p in plane_to] + [other]
    greeted = [device(x, 3 - y, (z + d) % 8, core) for d in FAR_FIRST] + greeted
    greeted = [p[0] for p in z_to] + greeted
    for target in greeted:
        pl.semaphore_signal(barrier, inc=1, device_id=target, device_id_type=MESH)

    small = [
        pltpu.make_async_copy(src, dst, in_sems.at[i])
        for i, (src, dst) in enumerate(((w_hbm, w_ref), (id_hbm, id_ref), (q_hbm, q_ref)))
    ]
    for copy in small:
        copy.start()
    load = pltpu.make_async_copy(pas_ref, pas.at[0], pas_sem.at[0])
    load.start()
    for copy in small:
        copy.wait()

    weights = w_ref[...].astype(F32)
    weight_sum = jnp.sum(weights, axis=1, keepdims=True)
    own_prob = weights / weight_sum
    entropy = jnp.sum(own_prob * jnp.log(own_prob), axis=1, keepdims=True)
    pad = 256 - num_cand
    wide_w = jnp.concatenate([weights, jnp.zeros((16, pad), F32)], axis=1)
    wide_id = jnp.concatenate([id_ref[...], jnp.zeros((16, pad), I32)], axis=1)
    s1, s2, s3 = split3(weight_sum)
    lane32 = iota((16, 32), 1)
    sums = jnp.where(
        lane32 == 0,
        s1.astype(F32),
        jnp.where(lane32 == 1, s2.astype(F32), jnp.where(lane32 == 2, s3.astype(F32), 0.0)),
    )
    for zz in range(8):
        lo = per_plane * zz
        ids = jnp.maximum(wide_id[:, lo : lo + 32] - lo * stride, 0)
        high = (ids >> 8).astype(F32)
        low = (ids & 255).astype(F32)
        cand_out[zz] = jnp.concatenate([high, low, wide_w[:, lo : lo + 32], sums], axis=1).astype(BF16)
    cands[0] = cand_out[z]
    queries[0] = q_ref[...]

    pl.semaphore_wait(barrier, len(greeted))

    swap = pltpu.make_async_remote_copy(
        pas_ref, pas.at[1], pas_sem.at[1], pas_sem.at[2], device_id=other, device_id_type=MESH
    )
    swap.start()
    sent = []
    mirror = device(x, 3 - y, z, core)

    def send(src, dst, sems, i, target):
        copy = pltpu.make_async_remote_copy(
            src, dst, sems.at[0, i], sems.at[1, i], device_id=target, device_id_type=MESH
        )
        copy.start()
        sent.append(copy)
        return copy

    cand_copies, near_copies, low_copies, high_copies = [], {}, [], []
    for d in FAR_FIRST + (0,):
        for dy in (0, 1):
            if d or dy:
                target = device(x, 3 - y if dy else y, (z + d) % 8, core)
                slot = dy * 8 + (8 - d) % 8
                cand_copies.append(send(cand_out.at[(z + d) % 8], cands.at[slot], c_sems, slot, target))
    for d in RELAYED:
        target = device(x, y, (z + d) % 8, core)
        near_copies[d] = send(q_ref, queries.at[8 - d], q_sems, d, target)
    for d in DIRECT:
        target = device(x, 3 - y, (z + d) % 8, core)
        high_copies.append(send(q_ref, queries.at[16 - d], q_sems, 8 + d, target))
    high_copies.append(send(q_ref, queries.at[8], q_sems, 8, mirror))
    for d in DIRECT:
        target = device(x, y, (z + d) % 8, core)
        low_copies.append(send(q_ref, queries.at[8 - d], q_sems, d, target))
    p_row = iota((128, 1), 0)
    p_x = (x + (p_row >> 5)) & 3
    p_y = (y_lo + ((p_row >> 4) & 1)) & 1
    p_n = ((p_row >> 1) & 7) * 16 + (p_x * 2 + p_y) * 2 + (p_row & 1)
    mask = iota((128, 128), 1) == p_n
    perm_ref[...] = mask.astype(F32).astype(BF16)

    offsets = [((((z * 2 + y_hi) * 2 + c) * 8) + slab) * width for c in (core, 1 - core)]
    firsts = [jnp.minimum(off // stride, num_cand - 2) - per_plane * z for off in offsets]
    out_lane = iota((1, 128), 1)
    target_lane = jnp.where((out_lane >= 12) & (out_lane < 15), 96 + out_lane - 12, -1)
    for rho in range(2):
        for c in range(2):
            for field in range(3):
                target_lane = jnp.where(
                    out_lane == (rho * 2 + c) * 3 + field, field * 32 + firsts[rho] + c, target_lane
                )
    pick = (iota((128, 128), 0) == target_lane).astype(F32).astype(BF16)
    load.wait()
    pas_t[0] = pas[0].T
    for copy in cand_copies:
        copy.wait_recv()
    picked = jnp.dot(cands[...].reshape(256, 128), pick, preferred_element_type=F32).astype(BF16)
    picked = jnp.concatenate(
        [
            jnp.dot(perm_ref[...], picked[h * 128 : h * 128 + 128], preferred_element_type=F32)
            for h in range(2)
        ],
        axis=0,
    )
    total_w = picked[:, 12:13] + picked[:, 13:14] + picked[:, 14:15]
    for d in RELAYED:
        near_copies[d].wait_recv()
        high_copies.append(send(queries.at[8 - d], queries.at[16 - d], q_sems, 8 + d, mirror))

    swap.wait_recv()
    pas_t[1] = pas[1].T

    column = iota((128, width), 1).astype(F32)
    prob_copies, prob_sums = [], []
    for h in range(2):
        mine = slice(h * 128, h * 128 + 128)
        prob_sum = None
        for rho in range(2):
            shift = (per_plane * stride * z - offsets[rho]).astype(F32)
            dense = 0.0
            for c in range(2):
                at = (rho * 2 + c) * 3
                local = picked[mine, at : at + 1] * 256.0 + picked[mine, at + 1 : at + 2] + shift
                prob = picked[mine, at + 2 : at + 3] / total_w[mine]
                dense = jnp.where(column == local, prob, dense)
            part = jnp.dot(dense.astype(BF16), pas[rho], preferred_element_type=F32)
            prob_sum = part if prob_sum is None else prob_sum + part
        prob_sums.append(prob_sum)
        groups = prob_sum.astype(BF16).reshape(4, 2, 16, -1)
        span = pl.ds(h * 2, 2)
        for ex in (2, 1, 3, 0):
            prob_out[ex, span] = groups[ex]
            if ex:
                target = device((x + ex) % 4, y, z, core)
                prob_copies.append(
                    send(prob_out.at[ex, span], prob_in.at[4 - ex, span], prob_sems, ex + 4 * h, target)
                )

    depth = q_ref.shape[1]
    exp_copies, stat_copies = [], []
    for h, waits in ((1, high_copies), (0, low_copies)):
        for copy in waits:
            copy.wait_recv()
        half = queries[h * 8 : h * 8 + 8].reshape(128, depth)
        rows = jnp.dot(perm_ref[...], half, preferred_element_type=F32)
        rows16 = rows.astype(BF16)
        scores = [
            scale * jnp.dot(rows16, pas_t[rho], preferred_element_type=F32)
            for rho in range(2)
        ]
        peak = jnp.maximum(
            jnp.max(scores[0], axis=1, keepdims=True), jnp.max(scores[1], axis=1, keepdims=True)
        )
        exps = [jnp.exp(s - peak) for s in scores]
        mixed = jnp.dot(exps[0].astype(BF16), pas[0], preferred_element_type=F32) + jnp.dot(
            exps[1].astype(BF16), pas[1], preferred_element_type=F32
        )
        exp_out[h * 8 : h * 8 + 8] = mixed.astype(BF16).reshape(8, 16, depth)
        for i, (target, group, slot) in enumerate(plane_to):
            if group // 8 == h:
                exp_copies.append(send(exp_out.at[group], exp_in.at[slot], exp_sems, i, target))
        total = jnp.sum(exps[0], axis=1, keepdims=True) + jnp.sum(exps[1], axis=1, keepdims=True)
        teacher = scale * jnp.sum(rows * prob_sums[h], axis=1, keepdims=True)
        for k, stat in enumerate((peak, total, teacher)):
            stat_out[h, k : k + 1, :] = jnp.sum(jnp.where(mask, stat, 0.0), axis=0, keepdims=True)
        for i, (target, group, slot) in enumerate(plane_to):
            if group // 8 == h:
                stat_copies.append(send(stat_out.at[h], stat_in.at[slot], stat_sems, i, target))

    stat_in[0] = stat_out[0]
    o = iota((384, 1), 0)
    d_of = o // 48
    j = o - 48 * d_of
    part = j // 12
    jj = j - 12 * part
    source = part * 96 + (jj >> 1) * 16 + d_of * 2 + (jj & 1)
    order = (iota((384, 384), 1) == source).astype(F32).astype(BF16)
    entropy_lanes = jnp.sum(
        jnp.where(iota((16, 16), 0) == iota((16, 16), 1), entropy, 0.0), axis=0, keepdims=True
    )
    for copy in prob_copies:
        copy.wait_recv()
    prob_rows = prob_out[0].astype(F32)
    for i in range(1, 4):
        prob_rows = prob_rows + prob_in[i].astype(F32)
    line_out[...] = prob_rows.astype(BF16)
    prob_rows = prob_rows[0]
    line_copies = []
    for k in (2, 3, 1):
        target = device(x, ((y_hi + k // 2) % 2) * 2 + (y_lo + k % 2) % 2, z, core)
        line_copies.append(send(line_out.at[k], line_in.at[k], prob_sems, 7 + k, target))
    for copy in stat_copies:
        copy.wait_recv()
    peaks = jnp.concatenate([stat_in[i, 0:1, :] for i in range(16)], axis=0)
    totals = jnp.concatenate([stat_in[i, 1:2, :] for i in range(16)], axis=0)
    teachers = jnp.concatenate([stat_in[i, 2:3, :] for i in range(16)], axis=0)
    peak = jnp.max(peaks, axis=0, keepdims=True)
    share = jnp.exp(peaks - peak)
    total = jnp.sum(totals * share, axis=0, keepdims=True)
    teacher = jnp.sum(teachers, axis=0, keepdims=True)
    zstat_out[0:1, :] = peak
    zstat_out[1:2, :] = total
    zstat_out[2:3, :] = teacher
    zstat_copies = [
        send(zstat_out, zstat_in.at[slot], zstat_sems, i, target)
        for i, (target, d, slot) in enumerate(z_to)
    ]
    row = iota((16, 128), 0)
    own_lane = iota((16, 128), 1) == (row >> 1) * 16 + slab * 2 + (row & 1)
    columns = [
        jnp.sum(jnp.where(own_lane, share[i : i + 1, :], 0.0), axis=1, keepdims=True) for i in range(16)
    ]
    exp_rows = exp_out[0].astype(F32) * columns[0]
    for copy, (_, _, slot) in zip(exp_copies, plane_to[7:] + plane_to[:7]):
        copy.wait_recv()
        exp_rows = exp_rows + exp_in[slot].astype(F32) * columns[slot]

    for copy in line_copies:
        copy.wait_recv()
    for k in range(1, 4):
        prob_rows = prob_rows + line_in[k].astype(F32)

    stacked = jnp.concatenate(
        [part[:, b * 128 : (b + 1) * 128] for part in (exp_rows, prob_rows) for b in range(6)], axis=0
    )
    coarse = stacked.astype(BF16)
    fine = (stacked - coarse.astype(F32)).astype(BF16)
    stacked = jnp.concatenate([coarse, fine], axis=0)
    z_out[...] = jnp.dot(order, stacked, preferred_element_type=F32).astype(BF16).reshape(8, 48, 128)
    z_copies = [
        send(z_out.at[d], z_in.at[slot], z_sems, i, target) for i, (target, d, slot) in enumerate(z_to)
    ]

    zstat_in[0] = zstat_out[...]
    for copy in zstat_copies:
        copy.wait_recv()

    def gathered(k):
        return jnp.concatenate(
            [zstat_in[s, k : k + 1, ((8 - s) % 8) * 16 : ((8 - s) % 8) * 16 + 16] for s in range(8)], axis=0
        )

    peaks, totals, teachers = gathered(0), gathered(1), gathered(2)
    peak = jnp.max(peaks, axis=0, keepdims=True)
    total = jnp.sum(totals * jnp.exp(peaks - peak), axis=0, keepdims=True)
    lse = peak + jnp.log(total)
    loss_ref[...] = entropy_lanes - jnp.sum(teachers, axis=0, keepdims=True) + lse
    share = jnp.exp(peaks - lse)
    row = iota((16, 16), 0)
    own_lane = iota((16, 16), 1) == slab * 2 + (row & 1)
    columns = [
        jnp.sum(jnp.where(own_lane, share[s : s + 1, :], 0.0), axis=1, keepdims=True) for s in range(8)
    ]
    for copy in z_copies:
        copy.wait_recv()
    z_in[0] = z_out[0]
    result = None
    for s in range(8):
        block = z_in[s].astype(F32)
        block = block[0:24] + block[24:48]
        term = block[0:12] * columns[s][0:12] - block[12:24]
        result = term if result is None else result + term
    result = scale * result
    for b in range(6):
        grad_ref[:, b * 128 : (b + 1) * 128] = result[2 * b : 2 * b + 2]

    swap.wait_send()
    for copy in sent:
        copy.wait_send()


def shards(queries, teacher_weight, cand_ids, passages):
    rows, depth = queries.shape
    width = passages.shape[0]
    num_cand = cand_ids.shape[1]
    stride = width * 256 // num_cand
    scale = 3.0 / math.sqrt(depth)
    vmem = pl.BlockSpec(memory_space=pltpu.VMEM)
    dma = pltpu.SemaphoreType.DMA
    loss, grad = pl.pallas_call(
        functools.partial(kernel, stride, scale),
        out_shape=(pltpu.VMEM((1, rows), F32), pltpu.VMEM((2, depth), F32)),
        in_specs=[pl.BlockSpec(memory_space=pltpu.HBM)] * 4,
        out_specs=(vmem, vmem),
        scratch_shapes=[
            pltpu.VMEM((rows, depth), BF16),
            pltpu.VMEM((rows, num_cand), BF16),
            pltpu.VMEM((rows, num_cand), I32),
            pltpu.VMEM((2, width, depth), BF16),
            pltpu.VMEM((2, depth, width), BF16),
            pltpu.VMEM((16, 16, depth), BF16),
            pltpu.VMEM((16, 16, 128), BF16),
            pltpu.VMEM((8, 16, 128), BF16),
            pltpu.VMEM((128, 128), BF16),
            pltpu.VMEM((4, 4, 16, depth), BF16),
            pltpu.VMEM((16, 16, depth), BF16),
            pltpu.VMEM((2, 8, 128), F32),
            pltpu.VMEM((4, 4, 16, depth), BF16),
            pltpu.VMEM((4, 16, depth), BF16),
            pltpu.VMEM((4, 16, depth), BF16),
            pltpu.VMEM((16, 16, depth), BF16),
            pltpu.VMEM((16, 8, 128), F32),
            pltpu.VMEM((8, 48, 128), BF16),
            pltpu.VMEM((8, 48, 128), BF16),
            pltpu.VMEM((8, 128), F32),
            pltpu.VMEM((8, 8, 128), F32),
            dma((3,)),
            dma((3,)),
            dma((2, 16)),
            dma((2, 16)),
            dma((2, 15)),
            dma((2, 15)),
            dma((2, 15)),
            dma((2, 7)),
            dma((2, 7)),
        ],
        compiler_params=pltpu.CompilerParams(
            collective_id=0, has_side_effects=True, vmem_limit_bytes=60 * 1024 * 1024
        ),
    )(*(pltpu.with_memory_space_constraint(a, pltpu.HBM) for a in (queries, teacher_weight, cand_ids, passages)))
    return (loss.reshape(rows), grad)


def solution(mesh):
    return jax.shard_map(
        shards,
        mesh=mesh,
        in_specs=(P("blk", None), P("blk", None), P("blk", None), P(("blk", "slab"), None)),
        out_specs=(P("blk"), P(("blk", "slab"), None)),
        check_vma=False,
    )
```

```python
import functools
import math

import jax
import jax.numpy as jnp
from jax import lax
from jax.experimental import pallas as pl
from jax.experimental.pallas import tpu as pltpu
from jax.sharding import PartitionSpec as P

MESH = pl.DeviceIdType.MESH
F32 = jnp.float32
BF16 = jnp.bfloat16
I32 = jnp.int32
FAR_FIRST = (4, 3, 5, 2, 6, 1, 7)
RELAYED = (2, 6)
DIRECT = (1, 7, 4, 3, 5)


def position():
    blk = lax.axis_index("blk")
    slab = lax.axis_index("slab")
    z = blk // 4
    y = ((blk // 2) % 2) * 2 + slab % 2
    return slab // 2, y, z, blk % 2


def device(x, y, z, core):
    return {"blk": (z * 2 + y // 2) * 2 + core, "slab": x * 2 + y % 2}


def iota(shape, dim):
    return lax.broadcasted_iota(I32, shape, dim)


def split3(value):
    first = value.astype(BF16)
    rest = value - first.astype(F32)
    second = rest.astype(BF16)
    third = (rest - second.astype(F32)).astype(BF16)
    return first, second, third


def kernel(
    stride,
    scale,
    q_hbm,
    w_hbm,
    id_hbm,
    pas_ref,
    loss_ref,
    grad_ref,
    q_ref,
    w_ref,
    id_ref,
    pas,
    pas_t,
    queries,
    cands,
    cand_out,
    perm_ref,
    prob_out,
    exp_out,
    stat_out,
    prob_in,
    line_out,
    line_in,
    exp_in,
    stat_in,
    z_out,
    z_in,
    zstat_out,
    zstat_in,
    in_sems,
    pas_sem,
    q_sems,
    c_sems,
    prob_sems,
    exp_sems,
    stat_sems,
    z_sems,
    zstat_sems,
):
    x, y, z, core = position()
    y_hi, y_lo = y // 2, y % 2
    slab = x * 2 + y_lo
    width = pas_ref.shape[0]
    num_cand = id_ref.shape[1]
    plane = width * 32
    per_plane = plane // stride

    plane_to = [
        (
            device((x + ex) % 4, ((y_hi + dy) % 2) * 2 + (y_lo + eyl) % 2, z, core),
            dy * 8 + ex * 2 + eyl,
            dy * 8 + ((4 - ex) % 4) * 2 + eyl,
        )
        for dy in (0, 1)
        for ex in (2, 1, 3, 0)
        for eyl in (1, 0)
        if (dy, ex, eyl) != (0, 0, 0)
    ]
    z_to = [(device(x, y, (z + d) % 8, core), d, (8 - d) % 8) for d in FAR_FIRST]
    other = device(x, y, z, 1 - core)

    barrier = pltpu.get_barrier_semaphore()
    greeted = [p[0] for p in plane_to] + [other]
    greeted = [device(x, 3 - y, (z + d) % 8, core) for d in FAR_FIRST] + greeted
    greeted = [p[0] for p in z_to] + greeted
    for target in greeted:
        pl.semaphore_signal(barrier, inc=1, device_id=target, device_id_type=MESH)

    small = [
        pltpu.make_async_copy(src, dst, in_sems.at[i])
        for i, (src, dst) in enumerate(((w_hbm, w_ref), (id_hbm, id_ref), (q_hbm, q_ref)))
    ]
    for copy in small:
        copy.start()
    load = pltpu.make_async_copy(pas_ref, pas.at[0], pas_sem.at[0])
    load.start()
    for copy in small:
        copy.wait()

    weights = w_ref[...].astype(F32)
    weight_sum = jnp.sum(weights, axis=1, keepdims=True)
    own_prob = weights / weight_sum
    entropy = jnp.sum(own_prob * jnp.log(own_prob), axis=1, keepdims=True)
    pad = 256 - num_cand
    wide_w = jnp.concatenate([weights, jnp.zeros((16, pad), F32)], axis=1)
    wide_id = jnp.concatenate([id_ref[...], jnp.zeros((16, pad), I32)], axis=1)
    s1, s2, s3 = split3(weight_sum)
    lane32 = iota((16, 32), 1)
    sums = jnp.where(
        lane32 == 0,
        s1.astype(F32),
        jnp.where(lane32 == 1, s2.astype(F32), jnp.where(lane32 == 2, s3.astype(F32), 0.0)),
    )
    for zz in range(8):
        lo = per_plane * zz
        ids = jnp.maximum(wide_id[:, lo : lo + 32] - lo * stride, 0)
        high = (ids >> 8).astype(F32)
        low = (ids & 255).astype(F32)
        cand_out[zz] = jnp.concatenate([high, low, wide_w[:, lo : lo + 32], sums], axis=1).astype(BF16)
    cands[0] = cand_out[z]
    queries[0] = q_ref[...]

    pl.semaphore_wait(barrier, len(greeted))

    swap = pltpu.make_async_remote_copy(
        pas_ref, pas.at[1], pas_sem.at[1], pas_sem.at[2], device_id=other, device_id_type=MESH
    )
    swap.start()
    sent = []
    mirror = device(x, 3 - y, z, core)

    def send(src, dst, sems, i, target):
        copy = pltpu.make_async_remote_copy(
            src, dst, sems.at[0, i], sems.at[1, i], device_id=target, device_id_type=MESH
        )
        copy.start()
        sent.append(copy)
        return copy

    cand_copies, near_copies, low_copies, high_copies = [], {}, [], []
    for d in FAR_FIRST + (0,):
        for dy in (0, 1):
            if d or dy:
                target = device(x, 3 - y if dy else y, (z + d) % 8, core)
                slot = dy * 8 + (8 - d) % 8
                cand_copies.append(send(cand_out.at[(z + d) % 8], cands.at[slot], c_sems, slot, target))
    for d in RELAYED:
        target = device(x, y, (z + d) % 8, core)
        near_copies[d] = send(q_ref, queries.at[8 - d], q_sems, d, target)
    for d in DIRECT:
        target = device(x, 3 - y, (z + d) % 8, core)
        high_copies.append(send(q_ref, queries.at[16 - d], q_sems, 8 + d, target))
    high_copies.append(send(q_ref, queries.at[8], q_sems, 8, mirror))
    for d in DIRECT:
        target = device(x, y, (z + d) % 8, core)
        low_copies.append(send(q_ref, queries.at[8 - d], q_sems, d, target))
    p_row = iota((128, 1), 0)
    p_x = (x + (p_row >> 5)) & 3
    p_y = (y_lo + ((p_row >> 4) & 1)) & 1
    p_n = ((p_row >> 1) & 7) * 16 + (p_x * 2 + p_y) * 2 + (p_row & 1)
    mask = iota((128, 128), 1) == p_n
    perm_ref[...] = mask.astype(F32).astype(BF16)

    offsets = [((((z * 2 + y_hi) * 2 + c) * 8) + slab) * width for c in (core, 1 - core)]
    firsts = [jnp.minimum(off // stride, num_cand - 2) - per_plane * z for off in offsets]
    out_lane = iota((1, 128), 1)
    target_lane = jnp.where((out_lane >= 12) & (out_lane < 15), 96 + out_lane - 12, -1)
    for rho in range(2):
        for c in range(2):
            for field in range(3):
                target_lane = jnp.where(
                    out_lane == (rho * 2 + c) * 3 + field, field * 32 + firsts[rho] + c, target_lane
                )
    pick = (iota((128, 128), 0) == target_lane).astype(F32).astype(BF16)
    load.wait()
    pas_t[0] = pas[0].T
    for copy in cand_copies:
        copy.wait_recv()
    picked = jnp.dot(cands[...].reshape(256, 128), pick, preferred_element_type=F32).astype(BF16)
    picked = jnp.concatenate(
        [
            jnp.dot(perm_ref[...], picked[h * 128 : h * 128 + 128], preferred_element_type=F32)
            for h in range(2)
        ],
        axis=0,
    )
    total_w = picked[:, 12:13] + picked[:, 13:14] + picked[:, 14:15]
    for d in RELAYED:
        near_copies[d].wait_recv()
        high_copies.append(send(queries.at[8 - d], queries.at[16 - d], q_sems, 8 + d, mirror))

    swap.wait_recv()
    pas_t[1] = pas[1].T

    column = iota((128, width), 1).astype(F32)
    prob_copies, prob_sums = [], {}
    for h in (1, 0):
        mine = slice(h * 128, h * 128 + 128)
        prob_sum = None
        for rho in range(2):
            shift = (per_plane * stride * z - offsets[rho]).astype(F32)
            dense = 0.0
            for c in range(2):
                at = (rho * 2 + c) * 3
                local = picked[mine, at : at + 1] * 256.0 + picked[mine, at + 1 : at + 2] + shift
                prob = picked[mine, at + 2 : at + 3] / total_w[mine]
                dense = jnp.where(column == local, prob, dense)
            part = jnp.dot(dense.astype(BF16), pas[rho], preferred_element_type=F32)
            prob_sum = part if prob_sum is None else prob_sum + part
        prob_sums[h] = prob_sum
        groups = prob_sum.astype(BF16).reshape(4, 2, 16, -1)
        span = pl.ds(h * 2, 2)
        for ex in (2, 1, 3, 0):
            prob_out[ex, span] = groups[ex]
            if ex:
                target = device((x + ex) % 4, y, z, core)
                prob_copies.append(
                    send(prob_out.at[ex, span], prob_in.at[4 - ex, span], prob_sems, ex + 4 * h, target)
                )

    depth = q_ref.shape[1]
    exp_copies, stat_copies = [], []
    for h, waits in ((1, high_copies), (0, low_copies)):
        for copy in waits:
            copy.wait_recv()
        half = queries[h * 8 : h * 8 + 8].reshape(128, depth)
        rows = jnp.dot(perm_ref[...], half, preferred_element_type=F32)
        rows16 = rows.astype(BF16)
        scores = [
            scale * jnp.dot(rows16, pas_t[rho], preferred_element_type=F32)
            for rho in range(2)
        ]
        peak = jnp.maximum(
            jnp.max(scores[0], axis=1, keepdims=True), jnp.max(scores[1], axis=1, keepdims=True)
        )
        exps = [jnp.exp(s - peak) for s in scores]
        mixed = jnp.dot(exps[0].astype(BF16), pas[0], preferred_element_type=F32) + jnp.dot(
            exps[1].astype(BF16), pas[1], preferred_element_type=F32
        )
        exp_out[h * 8 : h * 8 + 8] = mixed.astype(BF16).reshape(8, 16, depth)
        for i, (target, group, slot) in enumerate(plane_to):
            if group // 8 == h:
                exp_copies.append(send(exp_out.at[group], exp_in.at[slot], exp_sems, i, target))
        total = jnp.sum(exps[0], axis=1, keepdims=True) + jnp.sum(exps[1], axis=1, keepdims=True)
        teacher = scale * jnp.sum(rows * prob_sums[h], axis=1, keepdims=True)
        for k, stat in enumerate((peak, total, teacher)):
            stat_out[h, k : k + 1, :] = jnp.sum(jnp.where(mask, stat, 0.0), axis=0, keepdims=True)
        for i, (target, group, slot) in enumerate(plane_to):
            if group // 8 == h:
                stat_copies.append(send(stat_out.at[h], stat_in.at[slot], stat_sems, i, target))

    stat_in[0] = stat_out[0]
    o = iota((384, 1), 0)
    d_of = o // 48
    j = o - 48 * d_of
    part = j // 12
    jj = j - 12 * part
    source = part * 96 + (jj >> 1) * 16 + d_of * 2 + (jj & 1)
    order = (iota((384, 384), 1) == source).astype(F32).astype(BF16)
    entropy_lanes = jnp.sum(
        jnp.where(iota((16, 16), 0) == iota((16, 16), 1), entropy, 0.0), axis=0, keepdims=True
    )
    for copy in prob_copies:
        copy.wait_recv()
    prob_rows = prob_out[0].astype(F32)
    for i in range(1, 4):
        prob_rows = prob_rows + prob_in[i].astype(F32)
    line_out[...] = prob_rows.astype(BF16)
    prob_rows = prob_rows[0]
    line_copies = []
    for k in (2, 3, 1):
        target = device(x, ((y_hi + k // 2) % 2) * 2 + (y_lo + k % 2) % 2, z, core)
        line_copies.append(send(line_out.at[k], line_in.at[k], prob_sems, 7 + k, target))
    for copy in stat_copies:
        copy.wait_recv()
    peaks = jnp.concatenate([stat_in[i, 0:1, :] for i in range(16)], axis=0)
    totals = jnp.concatenate([stat_in[i, 1:2, :] for i in range(16)], axis=0)
    teachers = jnp.concatenate([stat_in[i, 2:3, :] for i in range(16)], axis=0)
    peak = jnp.max(peaks, axis=0, keepdims=True)
    share = jnp.exp(peaks - peak)
    total = jnp.sum(totals * share, axis=0, keepdims=True)
    teacher = jnp.sum(teachers, axis=0, keepdims=True)
    zstat_out[0:1, :] = peak
    zstat_out[1:2, :] = total
    zstat_out[2:3, :] = teacher
    zstat_copies = [
        send(zstat_out, zstat_in.at[slot], zstat_sems, i, target)
        for i, (target, d, slot) in enumerate(z_to)
    ]
    row = iota((16, 128), 0)
    own_lane = iota((16, 128), 1) == (row >> 1) * 16 + slab * 2 + (row & 1)
    columns = [
        jnp.sum(jnp.where(own_lane, share[i : i + 1, :], 0.0), axis=1, keepdims=True) for i in range(16)
    ]
    exp_rows = exp_out[0].astype(F32) * columns[0]
    for copy, (_, _, slot) in zip(exp_copies, plane_to[7:] + plane_to[:7]):
        copy.wait_recv()
        exp_rows = exp_rows + exp_in[slot].astype(F32) * columns[slot]

    for copy in line_copies:
        copy.wait_recv()
    for k in range(1, 4):
        prob_rows = prob_rows + line_in[k].astype(F32)

    stacked = jnp.concatenate(
        [part[:, b * 128 : (b + 1) * 128] for part in (exp_rows, prob_rows) for b in range(6)], axis=0
    )
    coarse = stacked.astype(BF16)
    fine = (stacked - coarse.astype(F32)).astype(BF16)
    stacked = jnp.concatenate([coarse, fine], axis=0)
    z_out[...] = jnp.dot(order, stacked, preferred_element_type=F32).astype(BF16).reshape(8, 48, 128)
    z_copies = [
        send(z_out.at[d], z_in.at[slot], z_sems, i, target) for i, (target, d, slot) in enumerate(z_to)
    ]

    zstat_in[0] = zstat_out[...]
    for copy in zstat_copies:
        copy.wait_recv()

    def gathered(k):
        return jnp.concatenate(
            [zstat_in[s, k : k + 1, ((8 - s) % 8) * 16 : ((8 - s) % 8) * 16 + 16] for s in range(8)], axis=0
        )

    peaks, totals, teachers = gathered(0), gathered(1), gathered(2)
    peak = jnp.max(peaks, axis=0, keepdims=True)
    total = jnp.sum(totals * jnp.exp(peaks - peak), axis=0, keepdims=True)
    lse = peak + jnp.log(total)
    loss_ref[...] = entropy_lanes - jnp.sum(teachers, axis=0, keepdims=True) + lse
    share = jnp.exp(peaks - lse)
    row = iota((16, 16), 0)
    own_lane = iota((16, 16), 1) == slab * 2 + (row & 1)
    columns = [
        jnp.sum(jnp.where(own_lane, share[s : s + 1, :], 0.0), axis=1, keepdims=True) for s in range(8)
    ]
    for copy in z_copies:
        copy.wait_recv()
    z_in[0] = z_out[0]
    result = None
    for s in range(8):
        block = z_in[s].astype(F32)
        block = block[0:24] + block[24:48]
        term = block[0:12] * columns[s][0:12] - block[12:24]
        result = term if result is None else result + term
    result = scale * result
    for b in range(6):
        grad_ref[:, b * 128 : (b + 1) * 128] = result[2 * b : 2 * b + 2]

    swap.wait_send()
    for copy in sent:
        copy.wait_send()


def shards(queries, teacher_weight, cand_ids, passages):
    rows, depth = queries.shape
    width = passages.shape[0]
    num_cand = cand_ids.shape[1]
    stride = width * 256 // num_cand
    scale = 3.0 / math.sqrt(depth)
    vmem = pl.BlockSpec(memory_space=pltpu.VMEM)
    dma = pltpu.SemaphoreType.DMA
    loss, grad = pl.pallas_call(
        functools.partial(kernel, stride, scale),
        out_shape=(pltpu.VMEM((1, rows), F32), pltpu.VMEM((2, depth), F32)),
        in_specs=[pl.BlockSpec(memory_space=pltpu.HBM)] * 4,
        out_specs=(vmem, vmem),
        scratch_shapes=[
            pltpu.VMEM((rows, depth), BF16),
            pltpu.VMEM((rows, num_cand), BF16),
            pltpu.VMEM((rows, num_cand), I32),
            pltpu.VMEM((2, width, depth), BF16),
            pltpu.VMEM((2, depth, width), BF16),
            pltpu.VMEM((16, 16, depth), BF16),
            pltpu.VMEM((16, 16, 128), BF16),
            pltpu.VMEM((8, 16, 128), BF16),
            pltpu.VMEM((128, 128), BF16),
            pltpu.VMEM((4, 4, 16, depth), BF16),
            pltpu.VMEM((16, 16, depth), BF16),
            pltpu.VMEM((2, 8, 128), F32),
            pltpu.VMEM((4, 4, 16, depth), BF16),
            pltpu.VMEM((4, 16, depth), BF16),
            pltpu.VMEM((4, 16, depth), BF16),
            pltpu.VMEM((16, 16, depth), BF16),
            pltpu.VMEM((16, 8, 128), F32),
            pltpu.VMEM((8, 48, 128), BF16),
            pltpu.VMEM((8, 48, 128), BF16),
            pltpu.VMEM((8, 128), F32),
            pltpu.VMEM((8, 8, 128), F32),
            dma((3,)),
            dma((3,)),
            dma((2, 16)),
            dma((2, 16)),
            dma((2, 15)),
            dma((2, 15)),
            dma((2, 15)),
            dma((2, 7)),
            dma((2, 7)),
        ],
        compiler_params=pltpu.CompilerParams(
            collective_id=0, has_side_effects=True, vmem_limit_bytes=60 * 1024 * 1024
        ),
    )(*(pltpu.with_memory_space_constraint(a, pltpu.HBM) for a in (queries, teacher_weight, cand_ids, passages)))
    return (loss.reshape(rows), grad)


def solution(mesh):
    return jax.shard_map(
        shards,
        mesh=mesh,
        in_specs=(P("blk", None), P("blk", None), P("blk", None), P(("blk", "slab"), None)),
        out_specs=(P("blk"), P(("blk", "slab"), None)),
        check_vma=False,
    )
```
